512 devices in a mesh: win: 16 (over y, x), tile: 32 (over z, core).
Axes of the slice: x: 4, y: 4, z: 16, core: 2. Of those that a mesh axis runs over, the one named last changes fastest.
Arguments:
- traj_start: float32 [16, 3, 2, 256, 1024], P('win', None, None, 'tile'), may hold values from -3 to 3
- forcing: float32 [3, 2, 256, 1024], P(None, None, 'tile'), may hold values from -3 to 3
- depth: float32 [2, 256, 1024], P(None, 'tile'), may hold values from 0.5 to 2
- obs_step: int32 [16, 256, 1024], P('win', 'tile'), may hold values from 0 to 6
- obs_value: float32 [16, 2, 256, 1024], P('win', None, 'tile'), may hold values from -4 to 4
- obs_weight: float32 [256, 1024], P('tile'), may hold values from 0.5 to 2
- error_weight: float32 [3, 2], replicated, may hold values from 0.5 to 2
Outputs:
- grad_start: float32 [16, 3, 2, 256, 1024], P('win', None, None, 'tile')
- grad_forcing: float32 [3, 2, 256, 1024], P(None, None, 'tile')
The draws below stay inside these ranges and needn't reach their ends.
Inputs may be any that keep to these rules, and one draw needn't show every extreme that they name: `obs_step`: 0 means that the cell is not observed in that sub-window; k >= 1 means that its thicknesses are observed after step k.
All inputs are finite; a program needn't handle non-finite values.
Results may differ from the reference program's by a relative error of at most 0.0003.
Values sent between devices are 32-bit elements; how exact they have to be, the bound alone decides.
A program may use at most 64 MiB of HBM per device.

```python
import math
import jax
import jax.numpy as jnp
from jax import lax

NX = 1024
LEV = 2
STEPS = 6
LAT_ROWS = 2048
SUBWIN = 16
NY = 256
BAND_START = 896


def touch_ends(result, own_key, low, top_value):
    longest = result.shape.index(max(result.shape))
    spots = []
    for shift in (0, 1):
        where = [jax.random.randint(jax.random.fold_in(own_key, axis), (), 0, length) for axis, length in enumerate(result.shape)]
        where[longest] = (where[longest] + shift) % result.shape[longest]
        spots.append(tuple(where))
    return result.at[spots[0]].set(low).at[spots[1]].set(top_value)


def block_levels(own_key, shape, shards, smallest, high):
    def one(position, shards_of):
        draws = jax.random.uniform(jax.random.fold_in(jax.random.fold_in(own_key, 6), position), (shards_of,), jnp.float32, smallest / len(shards), high / len(shards))
        return jnp.repeat(jnp.exp(draws), shape[position] // shards_of).reshape((-1,) + (1,) * (len(shape) - position - 1))

    gain = one(*shards[0])
    for cut in shards[1:]:
        gain = gain * one(*cut)
    return gain


def normal_values(key, shape, deviation, bound, pieces=(), kind=jnp.bfloat16):
    array = deviation * jax.random.normal(key, shape, jnp.float32)
    if pieces:
        array = array * block_levels(key, shape, pieces, -0.22, 0.18)
    return jnp.clip(array, -bound, bound).astype(kind)


def setup_inputs(seed: int = 0) -> dict:
    key_list = jax.random.split(jax.random.key(seed), 8)
    return {
        "traj_start": normal_values(key_list[0], (SUBWIN, 3, LEV, NY, NX), 0.5, 3.0, ((0, 16), (3, 32)), jnp.float32),
        "forcing": normal_values(key_list[1], (3, LEV, NY, NX), 0.3, 3.0, ((2, 32),), jnp.float32),
        "depth": jnp.clip(jnp.exp(math.log(2.0) - 1.3862944 * jax.random.uniform(key_list[2], (LEV, NY, NX), jnp.float32) ** block_levels(key_list[2], (LEV, NY, NX), ((1, 32),), -0.2, 0.2)), 0.5, 2.0),
        "obs_step": touch_ends(jax.random.randint(key_list[3], (SUBWIN, NY, NX), 0, STEPS + 1), jax.random.fold_in(key_list[3], 1), 0, STEPS).astype(jnp.int32),
        "obs_value": normal_values(key_list[4], (SUBWIN, LEV, NY, NX), 1.0, 4.0, ((0, 16), (2, 32)), jnp.float32),
        "obs_weight": jnp.clip(jnp.exp(math.log(2.0) - 1.3862944 * jax.random.uniform(key_list[5], (NY, NX), jnp.float32) ** block_levels(key_list[5], (NY, NX), ((0, 32),), -0.2, 0.2)), 0.5, 2.0),
        "error_weight": jnp.clip(jnp.exp(jax.random.uniform(key_list[6], (3, LEV), jnp.float32, math.log(0.5), math.log(2.0))), 0.5, 2.0),
    }


C_STEP = 0.2

def along_x(field):
    return 0.5 * (jnp.roll(field, -1, axis=-1) - jnp.roll(field, 1, axis=-1))

def along_y(field):
    return 0.5 * (field[:, 2:] - field[:, :-2])

def advance(padded, depth_pad, first_row, total_rows):
    zonal = padded[0]
    meridional = padded[1]
    height = padded[2]
    pressure = jnp.cumsum(height, axis=0)
    inner_rows = padded.shape[2] - 2
    latitude_rows = (first_row + 1 + jnp.arange(inner_rows, dtype=jnp.int32)).astype(jnp.float32)
    coriolis = (2.0 * jnp.sin(jnp.pi * ((latitude_rows + 0.5) / total_rows - 0.5)))[None, :, None]
    zonal_in = zonal[:, 1:-1]
    merid_in = meridional[:, 1:-1]
    height_in = height[:, 1:-1]
    column_mass = depth_pad + height
    new_zonal = zonal_in - C_STEP * (zonal_in * along_x(zonal_in) + merid_in * along_y(zonal) + along_x(pressure[:, 1:-1])) + C_STEP * coriolis * merid_in
    new_merid = merid_in - C_STEP * (zonal_in * along_x(merid_in) + merid_in * along_y(meridional) + along_y(pressure)) - C_STEP * coriolis * zonal_in
    new_height = height_in - C_STEP * (along_x((column_mass * zonal)[:, 1:-1]) + along_y(column_mass * meridional))
    return jnp.stack([new_zonal, new_merid, new_height])

def reference(traj_start, forcing, depth, obs_step, obs_value, obs_weight, error_weight):
    depth_pad = jnp.pad(depth, ((0, 0), (1, 1), (0, 0)))

    def pad_rows(state):
        return jnp.pad(state, ((0, 0), (0, 0), (1, 1), (0, 0)))

    def plain_step(state):
        return advance(pad_rows(state), depth_pad, BAND_START - 1, LAT_ROWS)

    def run_forward(initial):
        history = [initial]
        for step_index in range(STEPS):
            history.append(plain_step(history[-1]) + forcing)
        return history
    finals = lax.map(lambda initial: run_forward(initial)[-1], traj_start)
    weights = error_weight[None, :, :, None, None]
    misfit = weights * (traj_start[1:] - finals[:-1])
    misfit = jnp.concatenate([misfit, jnp.zeros_like(misfit[:1])], axis=0)
    earlier = jnp.concatenate([jnp.zeros_like(misfit[:1]), misfit[:-1]], axis=0)

    def sweep(packed):
        initial, observed, measured, mismatch = packed
        history = run_forward(initial)
        adjoint = -mismatch
        forcing_grad = jnp.zeros_like(adjoint)
        for step_index in range(STEPS, 0, -1):
            state_now = history[step_index]
            selected = (observed == step_index).astype(jnp.float32)
            pull_obs = obs_weight * selected * (state_now[2] - measured)
            adjoint = jnp.concatenate([adjoint[:2], (adjoint[2] + pull_obs)[None]], axis=0)
            forcing_grad = forcing_grad + adjoint
            unused, backward = jax.vjp(plain_step, history[step_index - 1])
            adjoint, = backward(adjoint)
        return (adjoint, forcing_grad)
    starts, grads = lax.map(sweep, (traj_start, obs_step, obs_value, misfit))
    return (starts + earlier, lax.optimization_barrier(jnp.sum(grads, axis=0)))
```

```python
import functools

import jax
import jax.numpy as jnp
from jax import lax
from jax.experimental import pallas as pl
from jax.experimental.pallas import tpu as pltpu
from jax.sharding import PartitionSpec as P

MESH = pl.DeviceIdType.MESH
STEPS = 6
LAT_ROWS = 2048
C_STEP = 0.2
HALF_C = 0.1
OWN = 8
PAD = 7
ROWS = OWN + 2 * PAD
NF = 6
SUB = 8
RW = NF * SUB


def along_x(a):
    ax = a.ndim - 1
    lane = lax.broadcasted_iota(jnp.int32, a.shape, ax)
    up = pltpu.roll(a, 127, ax)
    up = jnp.where(lane == 127, pltpu.roll(up, SUB - 1, ax - 1), up)
    down = pltpu.roll(a, 1, ax)
    down = jnp.where(lane == 0, pltpu.roll(down, 1, ax - 1), down)
    return up - down


def rows_of(ref, first, count, width):
    start = first * (width * SUB)
    if not isinstance(first, int):
        start = pl.multiple_of(start, SUB)
    return ref[pl.ds(start, count * width * SUB), :].reshape(count, width, SUB, 128)


def put_rows(ref, first, width, value):
    start = first * (width * SUB)
    if not isinstance(first, int):
        start = pl.multiple_of(start, SUB)
    count = value.shape[0]
    ref[pl.ds(start, count * width * SUB), :] = value.reshape(count * width * SUB, 128)


def kernel(
    win_n, tile_n, traj, forc, dep, ostep, oval, owt, ew,
    gs_out, gf_out,
    X, F, D, OS, OV, OW, COR, NXT, MU, EARL, LAM, G, GH, LH, RS, RED, AG,
    init_s, init_r, nxt_s, nxt_r, mu_s, mu_r, h_s, h_r, rs_s, rs_r, ag_s, ag_r,
):
    w = lax.axis_index("win")
    t = lax.axis_index("tile")
    y, x = w // 4, lax.rem(w, 4)

    def peer(a, b):
        return lax.rem(y + a, 4) * 4 + lax.rem(x + b, 4)

    peers = [(a, b) for a in range(4) for b in range(4) if a or b]
    peers.sort(key=lambda p: -(min(p[0], 4 - p[0]) + min(p[1], 4 - p[1])))

    barrier = pltpu.get_barrier_semaphore()
    for a, b in peers:
        pl.semaphore_signal(barrier, inc=1, device_id={"win": peer(a, b), "tile": t}, device_id_type=MESH)

    @pl.when(t > 0)
    def _():
        pl.semaphore_signal(barrier, inc=1, device_id={"win": w, "tile": t - 1}, device_id_type=MESH)

    @pl.when(t < tile_n - 1)
    def _():
        pl.semaphore_signal(barrier, inc=1, device_id={"win": w, "tile": t + 1}, device_id_type=MESH)

    for f in range(NF):
        for s in range(SUB):
            cols = pl.ds(128 * s, 128)
            X[0, pl.ds(PAD * RW + f * SUB + s, OWN, stride=RW), :] = traj[0, f // 2, f % 2, :, cols]
            F[pl.ds(PAD * RW + f * SUB + s, OWN, stride=RW), :] = forc[f // 2, f % 2, :, cols]
    for l in range(2):
        for s in range(SUB):
            cols = pl.ds(128 * s, 128)
            D[pl.ds(PAD * 16 + l * SUB + s, OWN, stride=16), :] = dep[l, :, cols]
            OV[pl.ds(PAD * 16 + l * SUB + s, OWN, stride=16), :] = oval[0, l, :, cols]
    for s in range(SUB):
        cols = pl.ds(128 * s, 128)
        OS[pl.ds(PAD * SUB + s, OWN, stride=SUB), :] = ostep[0, :, cols]
        OW[pl.ds(PAD * SUB + s, OWN, stride=SUB), :] = owt[:, cols]

    def clear(ref, first, count, width):
        ref[pl.ds(first * width * SUB, count * width * SUB), :] = jnp.zeros((count * width * SUB, 128), ref.dtype)

    for k in range(STEPS):
        for i in (k, ROWS - 1 - k):
            clear(X.at[k], i, 1, NF)
    clear(D, 0, 1, 2)
    clear(D, ROWS - 1, 1, 2)
    for i in (0, PAD + OWN):
        clear(OS, i, PAD, 1)
        clear(OW, i, PAD, 1)
        clear(OV, i, PAD, 2)
        clear(G, i, PAD, NF)
        clear(LAM.at[0], i, PAD, NF)
        clear(LAM.at[1], i, PAD, NF)

    @pl.when(t == 0)
    def _():
        clear(X.at[0], 1, PAD - 1, NF)
        clear(F, 1, PAD - 1, NF)
        clear(D, 1, PAD - 1, 2)

    @pl.when(t == tile_n - 1)
    def _():
        clear(X.at[0], PAD + OWN, PAD - 1, NF)
        clear(F, PAD + OWN, PAD - 1, NF)
        clear(D, PAD + OWN, PAD - 1, 2)

    band_row = lax.broadcasted_iota(jnp.int32, (24, 128), 0) + (t * OWN - PAD)
    lat = ((LAT_ROWS - tile_n * OWN) // 2 + band_row).astype(jnp.float32)
    COR[...] = (2.0 * C_STEP) * jnp.sin(jnp.pi * ((lat + 0.5) / LAT_ROWS - 0.5))

    def valid(i):
        row = t * OWN - PAD + i
        return jnp.where((row >= 0) & (row < tile_n * OWN), 1.0, 0.0)

    has_low = jnp.where(t > 0, 1, 0)
    has_high = jnp.where(t < tile_n - 1, 1, 0)
    pl.semaphore_wait(barrier, win_n - 1 + has_low + has_high)

    def halo(src, dst, src_row, dst_row, count, width, n, side, sems, tile):
        return pltpu.make_async_remote_copy(
            src_ref=src.at[pl.ds(src_row * width * SUB, count * width * SUB), :],
            dst_ref=dst.at[pl.ds(dst_row * width * SUB, count * width * SUB), :],
            send_sem=sems[0].at[n, side], recv_sem=sems[1].at[n, side],
            device_id={"win": w, "tile": tile}, device_id_type=MESH)

    init = (init_s, init_r)
    ups = [halo(X.at[0], X.at[0], PAD + 2, 1, 6, NF, 0, 0, init, t + 1),
           halo(D, D, PAD + 2, 1, 6, 2, 1, 0, init, t + 1),
           halo(F, F, PAD + 3, 2, 5, NF, 2, 0, init, t + 1)]
    downs = [halo(X.at[0], X.at[0], PAD, PAD + OWN, 6, NF, 0, 1, init, t - 1),
             halo(D, D, PAD, PAD + OWN, 6, 2, 1, 1, init, t - 1),
             halo(F, F, PAD, PAD + OWN, 5, NF, 2, 1, init, t - 1)]

    def to_tiles(ups, downs):
        @pl.when(t < tile_n - 1)
        def _():
            for c in ups:
                c.start()

        @pl.when(t > 0)
        def _():
            for c in downs:
                c.start()

    def from_tiles(ups, downs):
        @pl.when(t > 0)
        def _():
            for c in ups:
                c.wait_recv()

        @pl.when(t < tile_n - 1)
        def _():
            for c in downs:
                c.wait_recv()

    def sent_tiles(ups, downs):
        @pl.when(t < tile_n - 1)
        def _():
            for c in ups:
                c.wait_send()

        @pl.when(t > 0)
        def _():
            for c in downs:
                c.wait_send()

    to_tiles(ups, downs)
    nxt = pltpu.make_async_remote_copy(
        src_ref=X.at[0, pl.ds(PAD * RW, OWN * RW), :], dst_ref=NXT,
        send_sem=nxt_s, recv_sem=nxt_r, device_id={"win": w - 1, "tile": t}, device_id_type=MESH)

    @pl.when(w > 0)
    def _():
        nxt.start()

    from_tiles(ups, downs)

    NB = 2

    def forward(k):
        lo = k + 2

        def block(n, carry):
            i = lo + n * NB
            s = rows_of(X.at[k], i - 1, NB + 2, NF)
            m = rows_of(D, i - 1, NB + 2, 2)
            fo = rows_of(F, i, NB, NF)
            u, v, h = s[:, 0:2], s[:, 2:4], s[:, 4:6]
            p0 = h[:, 0]
            p1 = p0 + h[:, 1]
            mass = m + h
            r = mass * v
            for j in range(NB):
                cor = COR[pl.ds(i + j, 1), :]
                ok = valid(i + j)
                outs = []
                for l in range(2):
                    p = p1 if l else p0
                    uc, vc, hc = u[j + 1, l], v[j + 1, l], h[j + 1, l]
                    nu = uc - HALF_C * (uc * along_x(uc) + vc * (u[j + 2, l] - u[j, l]) + along_x(p[j + 1])) + cor * vc
                    nv = vc - HALF_C * (uc * along_x(vc) + vc * (v[j + 2, l] - v[j, l]) + (p[j + 2] - p[j])) - cor * uc
                    nh = hc - HALF_C * (along_x(mass[j + 1, l] * uc) + (r[j + 2, l] - r[j, l]))
                    outs.append((nu, nv, nh))
                for c in range(3):
                    for l in range(2):
                        f = 2 * c + l
                        put_rows(X.at[k + 1], (i + j) * NF + f, 1, ((outs[l][c] + fo[j, f]) * ok)[None])
            return carry

        lax.fori_loop(0, (ROWS - 2 * lo) // NB, block, 0)

    for k in range(STEPS):
        forward(k)

    not_last = jnp.where(w < win_n - 1, 1.0, 0.0)

    @pl.when(w < win_n - 1)
    def _():
        nxt.wait_recv()

    @pl.when(w == win_n - 1)
    def _():
        NXT[...] = X[STEPS, pl.ds(PAD * RW, OWN * RW), :]

    def end(i, carry):
        nx = rows_of(NXT, i, 1, NF)[0]
        last = rows_of(X.at[STEPS], PAD + i, 1, NF)[0]
        sel = rows_of(OS, PAD + i, 1, 1)[0, 0] == STEPS
        ov = rows_of(OV, PAD + i, 1, 2)[0]
        ow = jnp.where(sel, rows_of(OW, PAD + i, 1, 1)[0, 0], 0.0)
        for f in range(NF):
            mis = (ew[f // 2, f % 2] * not_last) * (nx[f] - last[f])
            put_rows(MU, i * NF + f, 1, mis[None])
            lam = -mis
            if f >= 4:
                lam = lam + ow * (last[f] - ov[f - 4])
            put_rows(LAM.at[0], (PAD + i) * NF + f, 1, lam[None])
            put_rows(G, (PAD + i) * NF + f, 1, lam[None])
        return carry

    lax.fori_loop(0, OWN, end, 0)
    mu = pltpu.make_async_remote_copy(
        src_ref=MU, dst_ref=EARL, send_sem=mu_s, recv_sem=mu_r,
        device_id={"win": w + 1, "tile": t}, device_id_type=MESH)

    @pl.when(w < win_n - 1)
    def _():
        mu.start()

    def backward(k):
        src, dst = (STEPS - k) % 2, (STEPS - k + 1) % 2
        lo = k

        def block(n, carry):
            i = lo + n * NB
            s = rows_of(X.at[k - 1], i - 1, NB + 2, NF)
            lam = rows_of(LAM.at[src], i - 1, NB + 2, NF)
            dp = rows_of(D, i, NB, 2)
            u, v, h = s[:, 0:2], s[:, 2:4], s[:, 4:6]
            a, b, c = lam[:, 0:2], lam[:, 2:4], lam[:, 4:6]
            va, vb = v * a, v * b
            if k > 1:
                os = rows_of(OS, i, NB, 1)
                ov = rows_of(OV, i, NB, 2)
                ow = rows_of(OW, i, NB, 1)
            for j in range(NB):
                cor = COR[pl.ds(i + j, 1), :]
                ok = valid(i + j)
                res = [None] * NF
                grads = []
                for l in range(2):
                    uc, vc, hc = u[j + 1, l], v[j + 1, l], h[j + 1, l]
                    ac, bc, cc = a[j + 1, l], b[j + 1, l], c[j + 1, l]
                    mass = dp[j, l] + hc
                    cx = along_x(cc)
                    cy = c[j + 2, l] - c[j, l]
                    res[l] = ac - cor * bc - HALF_C * (
                        ac * along_x(uc) + bc * along_x(vc) - along_x(uc * ac)
                        - (va[j + 2, l] - va[j, l]) - mass * cx)
                    res[2 + l] = bc + cor * ac - HALF_C * (
                        ac * (u[j + 2, l] - u[j, l]) + bc * (v[j + 2, l] - v[j, l]) - along_x(uc * bc)
                        - (vb[j + 2, l] - vb[j, l]) - mass * cy)
                    grads.append(along_x(ac) + (b[j + 2, l] - b[j, l]))
                    res[4 + l] = cc + HALF_C * (uc * cx + vc * cy)
                res[4] = res[4] + HALF_C * (grads[0] + grads[1])
                res[5] = res[5] + HALF_C * grads[1]
                if k > 1:
                    wt = jnp.where(os[j, 0] == k - 1, ow[j, 0], 0.0)
                    for l in range(2):
                        res[4 + l] = res[4 + l] + wt * (h[j + 1, l] - ov[j, l])
                for f in range(NF):
                    r = (res[f] * ok)[None]
                    put_rows(LAM.at[dst], (i + j) * NF + f, 1, r)
                    if k > 1:
                        old = rows_of(G, (i + j) * NF + f, 1, 1)[0]
                        put_rows(G, (i + j) * NF + f, 1, old + r)
            return carry

        lax.fori_loop(0, (ROWS - 2 * lo) // NB, block, 0)

    for k in range(STEPS, 0, -1):
        backward(k)

    hs = (h_s, h_r)
    gups = [halo(G, GH.at[0], PAD + OWN, 0, 5, NF, 0, 0, hs, t + 1)]
    gdowns = [halo(G, GH.at[1], PAD - 5, 0, 5, NF, 0, 1, hs, t - 1)]
    lups = [halo(LAM.at[0], LH.at[0], PAD + OWN, 0, 6, NF, 1, 0, hs, t + 1)]
    ldowns = [halo(LAM.at[0], LH.at[1], PAD - 6, 0, 6, NF, 1, 1, hs, t - 1)]
    to_tiles(gups + lups, gdowns + ldowns)
    from_tiles(gups, gdowns)

    def add_rows(ref, first, src, count):
        for i in range(count):
            put_rows(ref, first + i, NF, rows_of(ref, first + i, 1, NF) + rows_of(src, i, 1, NF))

    @pl.when(t > 0)
    def _():
        add_rows(G, PAD, GH.at[0], 5)

    @pl.when(t < tile_n - 1)
    def _():
        add_rows(G, PAD + 3, GH.at[1], 5)

    CH = OWN * RW // win_n
    sends = []
    for n, (a, b) in enumerate(peers):
        p = peer(a, b)
        c = pltpu.make_async_remote_copy(
            src_ref=G.at[pl.ds(pl.multiple_of(PAD * RW + p * CH, SUB), CH), :],
            dst_ref=RS.at[pl.ds(n * CH, CH), :],
            send_sem=rs_s.at[n], recv_sem=rs_r.at[n],
            device_id={"win": p, "tile": t}, device_id_type=MESH)
        c.start()
        sends.append(c)
    total = G[pl.ds(pl.multiple_of(PAD * RW + w * CH, SUB), CH), :]
    for c in sends:
        c.wait_recv()
    for n in range(win_n - 1):
        total = total + RS[pl.ds(n * CH, CH), :]
    RED[...] = total
    mine = pl.ds(pl.multiple_of(w * CH, SUB), CH)
    gathers = []
    for n, (a, b) in enumerate(peers):
        c = pltpu.make_async_remote_copy(
            src_ref=RED, dst_ref=AG.at[mine, :],
            send_sem=ag_s.at[n], recv_sem=ag_r.at[n],
            device_id={"win": peer(a, b), "tile": t}, device_id_type=MESH)
        c.start()
        gathers.append(c)
    AG[mine, :] = total

    from_tiles(lups, ldowns)
    first = LAM.at[0]

    @pl.when(t > 0)
    def _():
        add_rows(first, PAD, LH.at[0], 6)

    @pl.when(t < tile_n - 1)
    def _():
        add_rows(first, PAD + 2, LH.at[1], 6)

    @pl.when(w > 0)
    def _():
        mu.wait_recv()

    @pl.when(w == 0)
    def _():
        EARL[...] = jnp.zeros_like(EARL)

    for f in range(NF):
        for s in range(SUB):
            cols = pl.ds(128 * s, 128)
            gs_out[0, f // 2, f % 2, :, cols] = (
                first[pl.ds(PAD * RW + f * SUB + s, OWN, stride=RW), :]
                + EARL[pl.ds(f * SUB + s, OWN, stride=RW), :])

    for c in gathers:
        c.wait_recv()
    for f in range(NF):
        for s in range(SUB):
            gf_out[f // 2, f % 2, :, pl.ds(128 * s, 128)] = AG[pl.ds(f * SUB + s, OWN, stride=RW), :]

    sent_tiles(ups + gups + lups, downs + gdowns + ldowns)

    @pl.when(w > 0)
    def _():
        nxt.wait_send()

    @pl.when(w < win_n - 1)
    def _():
        mu.wait_send()

    for c in sends + gathers:
        c.wait_send()


def solution(mesh):
    win_n, tile_n = mesh.shape["win"], mesh.shape["tile"]

    def local(traj, forc, dep, ostep, oval, owt, ew):
        f32 = jnp.float32

        def flat(rows, width, dtype=f32, lead=()):
            return pltpu.VMEM(lead + (rows * width * SUB, 128), dtype)

        vm = pl.BlockSpec(memory_space=pltpu.VMEM)
        sem = pltpu.SemaphoreType.DMA
        return pl.pallas_call(
            functools.partial(kernel, win_n, tile_n),
            out_shape=(jax.ShapeDtypeStruct(traj.shape, f32), jax.ShapeDtypeStruct(forc.shape, f32)),
            in_specs=[vm] * 6 + [pl.BlockSpec(memory_space=pltpu.SMEM)],
            out_specs=(vm, vm),
            scratch_shapes=[
                flat(ROWS, NF, lead=(STEPS + 1,)),
                flat(ROWS, NF),
                flat(ROWS, 2),
                flat(ROWS, 1, jnp.int32),
                flat(ROWS, 2),
                flat(ROWS, 1),
                pltpu.VMEM((24, 128), f32),
                flat(OWN, NF),
                flat(OWN, NF),
                flat(OWN, NF),
                flat(ROWS, NF, lead=(2,)),
                flat(ROWS, NF),
                flat(5, NF, lead=(2,)),
                flat(6, NF, lead=(2,)),
                flat(OWN, NF),
                pltpu.VMEM((OWN * RW // win_n, 128), f32),
                flat(OWN, NF),
                sem((3, 2)), sem((3, 2)), sem, sem, sem, sem, sem((2, 2)), sem((2, 2)),
                sem((win_n - 1,)), sem((win_n - 1,)), sem((win_n - 1,)), sem((win_n - 1,)),
            ],
            compiler_params=pltpu.CompilerParams(
                collective_id=0, has_side_effects=True, vmem_limit_bytes=40 * 2**20),
        )(traj, forc, dep, ostep, oval, owt, ew)

    return jax.shard_map(
        local,
        mesh=mesh,
        in_specs=(
            P("win", None, None, "tile", None),
            P(None, None, "tile", None),
            P(None, "tile", None),
            P("win", "tile", None),
            P("win", None, "tile", None),
            P("tile", None),
            P(),
        ),
        out_specs=(P("win", None, None, "tile", None), P(None, None, "tile", None)),
        check_vma=False,
    )
```

```python
import functools

import jax
import jax.numpy as jnp
from jax import lax
from jax.experimental import pallas as pl
from jax.experimental.pallas import tpu as pltpu
from jax.sharding import PartitionSpec as P

MESH = pl.DeviceIdType.MESH
STEPS = 6
LAT_ROWS = 2048
C_STEP = 0.2
HALF_C = 0.1
OWN = 8
PAD = STEPS
ROWS = OWN + 2 * PAD
NF = 6
SUB = 8
RW = NF * SUB
BW = 14
BR = BW * SUB


def along_x(a):
    lane = lax.broadcasted_iota(jnp.int32, a.shape, 1)
    up = pltpu.roll(a, 127, 1)
    up = jnp.where(lane == 127, pltpu.roll(up, SUB - 1, 0), up)
    down = pltpu.roll(a, 1, 1)
    down = jnp.where(lane == 0, pltpu.roll(down, 1, 0), down)
    return up - down


def get(ref, row, f, width=NF):
    return ref[pl.ds((row * width + f) * SUB, SUB), :]


def put(ref, row, f, value, width=NF):
    ref[pl.ds((row * width + f) * SUB, SUB), :] = value


def less(a, b):
    if a is None:
        return None if b is None else -b
    return a if b is None else a - b


def kernel(
    win_n, tile_n, traj, forc, dep, ostep, oval, owt, ew,
    gs_out, gf_out,
    TT, TF, TD, TS, TV, TW,
    B0, X, DX, OS, OV, OW, COR, NT, NXT, MU, EARL, LAM, G, GH, LH, RS, RED, AG,
    in_s, init_s, init_r, nxt_s, nxt_r, mu_s, mu_r, h_s, h_r, rs_s, rs_r, ag_s, ag_r,
):
    w = lax.axis_index("win")
    t = lax.axis_index("tile")
    y, x = w // 4, lax.rem(w, 4)
    low_tile, high_tile = t > 0, t < tile_n - 1

    def peer(a, b):
        return lax.rem(y + a, 4) * 4 + lax.rem(x + b, 4)

    peers = [(a, b) for a in range(4) for b in range(4) if a or b]
    peers.sort(key=lambda p: -(min(p[0], 4 - p[0]) + min(p[1], 4 - p[1])))

    ins = [pltpu.make_async_copy(src, dst, in_s.at[n]) for n, (src, dst) in enumerate(
        [(traj.at[0], TT), (dep, TD), (forc, TF), (ostep.at[0], TS), (oval.at[0], TV), (owt, TW)])]
    for c in ins:
        c.start()

    barrier = pltpu.get_barrier_semaphore()

    def greet(win, tile):
        pl.semaphore_signal(barrier, inc=1, device_id={"win": win, "tile": tile}, device_id_type=MESH)

    for a, b in peers:
        greet(peer(a, b), t)

    @pl.when(low_tile)
    def _():
        greet(w, t - 1)

    @pl.when(high_tile)
    def _():
        greet(w, t + 1)

    band_row = lax.broadcasted_iota(jnp.int32, (24, 128), 0) + (t * OWN - PAD)
    lat = ((LAT_ROWS - tile_n * OWN) // 2 + band_row).astype(jnp.float32)
    COR[...] = (2.0 * C_STEP) * jnp.sin(jnp.pi * ((lat + 0.5) / LAT_ROWS - 0.5))
    low_ok = jnp.where(low_tile, 1.0, 0.0)
    high_ok = jnp.where(high_tile, 1.0, 0.0)

    @pl.when(t == 0)
    def _():
        B0[pl.ds(0, PAD * BR), :] = jnp.zeros((PAD * BR, 128), jnp.float32)

    @pl.when(t == tile_n - 1)
    def _():
        B0[pl.ds((PAD + OWN) * BR, PAD * BR), :] = jnp.zeros((PAD * BR, 128), jnp.float32)

    def spread(dst, first, width, f, tile):
        for s in range(SUB):
            dst[pl.ds((first * width + f) * SUB + s, OWN, stride=width * SUB), :] = tile(pl.ds(128 * s, 128))

    ins[0].wait()
    for f in range(NF):
        spread(B0, PAD, BW, f, lambda cols: TT[f // 2, f % 2, :, cols])
    ins[1].wait()
    for l in range(2):
        spread(B0, PAD, BW, 6 + l, lambda cols: TD[l, :, cols])
    ins[2].wait()
    for f in range(NF):
        spread(B0, PAD, BW, 8 + f, lambda cols: TF[f // 2, f % 2, :, cols])

    pl.semaphore_wait(barrier, win_n - 1 + jnp.where(low_tile, 1, 0) + jnp.where(high_tile, 1, 0))

    def to_tile(src, src_at, dst, dst_at, size, sems, n, side):
        return pltpu.make_async_remote_copy(
            src_ref=src.at[pl.ds(src_at, size), :], dst_ref=dst.at[pl.ds(dst_at, size), :],
            send_sem=sems[0].at[n, side], recv_sem=sems[1].at[n, side],
            device_id={"win": w, "tile": t + 1 if side == 0 else t - 1}, device_id_type=MESH)

    def init(n, near, count, size):
        up = (PAD + OWN - near - count + 1) * BR, (PAD - near - count + 1) * BR
        down = (PAD + near - 1) * BR, (PAD + OWN + near - 1) * BR
        return [to_tile(B0, a, B0, b, size, (init_s, init_r), n, side) for side, (a, b) in enumerate((up, down))]

    first = [init(0, 1, 2, 2 * BR), init(1, 3, 2, 2 * BR), init(2, 5, 1, BR), init(3, 6, 1, SUB * SUB)]

    def start(pairs):
        @pl.when(high_tile)
        def _():
            for c in pairs:
                c[0].start()

        @pl.when(low_tile)
        def _():
            for c in pairs:
                c[1].start()

    def arrive(pairs):
        @pl.when(low_tile)
        def _():
            for c in pairs:
                c[0].wait_recv()

        @pl.when(high_tile)
        def _():
            for c in pairs:
                c[1].wait_recv()

    def left(pairs):
        @pl.when(high_tile)
        def _():
            for c in pairs:
                c[0].wait_send()

        @pl.when(low_tile)
        def _():
            for c in pairs:
                c[1].wait_send()

    start(first)
    nxt = pltpu.make_async_remote_copy(
        src_ref=TT, dst_ref=NT, send_sem=nxt_s, recv_sem=nxt_r,
        device_id={"win": w - 1, "tile": t}, device_id_type=MESH)

    @pl.when(w > 0)
    def _():
        nxt.start()

    def state(k, r, f):
        return get(B0, PAD + r, f, BW) if k == 0 else get(X.at[k - 1], PAD + r, f)

    def side_ok(r):
        return low_ok if r < 0 else high_ok if r >= OWN else None

    def forward(k, blocks):
        outs = []
        for block in blocks:
            near = range(block[0] - 1, block[-1] + 2)
            s = {r: [state(k, r, f) for f in range(NF)] for r in near}
            p = {r: (s[r][4], s[r][4] + s[r][5]) for r in near}
            mass = {r: [get(B0, PAD + r, 6 + l, BW) + s[r][4 + l] for l in range(2)] for r in near}
            q = {r: [mass[r][l] * s[r][2 + l] for l in range(2)] for r in near}
            for r in block:
                cor = COR[pl.ds(PAD + r, 1), :]
                new, dx = [None] * NF, [None] * 4
                lo, hi = r - 1, r + 1
                for l in range(2):
                    u, v, h = s[r][l], s[r][2 + l], s[r][4 + l]
                    dx[l], dx[2 + l] = along_x(u), along_x(v)
                    new[l] = u - HALF_C * (u * dx[l] + v * (s[hi][l] - s[lo][l]) + along_x(p[r][l])) + cor * v
                    new[2 + l] = v - HALF_C * (
                        u * dx[2 + l] + v * (s[hi][2 + l] - s[lo][2 + l]) + (p[hi][l] - p[lo][l])) - cor * u
                    new[4 + l] = h - HALF_C * (along_x(mass[r][l] * u) + (q[hi][l] - q[lo][l]))
                ok = side_ok(r)
                for f in range(NF):
                    new[f] = new[f] + get(B0, PAD + r, 8 + f, BW)
                    if ok is not None:
                        new[f] = new[f] * ok
                outs.append((r, new, dx))
        for r, new, dx in outs:
            for f in range(NF):
                put(X.at[k], PAD + r, f, new[f])
            for f in range(4):
                put(DX.at[k], PAD + r, f, dx[f], 4)

    for k in range(3):
        forward(k, [range(1 + k, OWN - 1 - k)])
    for n, near in enumerate((1, 3, 5)):
        arrive([first[n]] if n < 2 else first[2:])
        if n == 0:
            for c in ins[3:]:
                c.wait()
            spread(OS, 0, 1, 0, lambda cols: TS[:, cols])
            spread(OW, 0, 1, 0, lambda cols: TW[:, cols])
            for l in range(2):
                spread(OV, 0, 2, l, lambda cols: TV[l, :, cols])
        for k in range(STEPS):
            low = [r for r in (k - near, k - near + 1) if r < OWN // 2]
            high = [OWN - 1 - r for r in reversed(low)]
            if low:
                forward(k, [low, high])

    not_last = jnp.where(w < win_n - 1, 1.0, 0.0)

    @pl.when(w < win_n - 1)
    def _():
        nxt.wait_recv()

    @pl.when(w == win_n - 1)
    def _():
        NT[...] = jnp.zeros_like(NT)

    for f in range(NF):
        spread(NXT, 0, NF, f, lambda cols: NT[f // 2, f % 2, :, cols])

    def pull(k, r, l):
        ow = jnp.where(get(OS, r, 0, 1) == k, get(OW, r, 0, 1), 0.0)
        return ow * (state(k, r, 4 + l) - get(OV, r, l, 2))

    for r in range(OWN):
        for f in range(NF):
            mis = (ew[f % 2, f // 2] * not_last) * (get(NXT, r, f) - state(STEPS, r, f))
            put(MU, r, f, mis)
            lam = -mis
            if f >= 4:
                lam = lam + pull(STEPS, r, f - 4)
            put(LAM.at[0], PAD + r, f, lam)
            put(G, PAD + r, f, lam)
    mu = pltpu.make_async_remote_copy(
        src_ref=MU, dst_ref=EARL, send_sem=mu_s, recv_sem=mu_r,
        device_id={"win": w + 1, "tile": t}, device_id_type=MESH)

    @pl.when(w < win_n - 1)
    def _():
        mu.start()

    def backward(k, rows):
        src, dst = LAM.at[(STEPS - k) % 2], LAM.at[(STEPS - k + 1) % 2]
        reach = STEPS - k
        none = [None] * NF
        near = range(rows[0] - 1, rows[-1] + 2)
        lam = {r: [get(src, PAD + r, f) for f in range(NF)] if -reach <= r < OWN + reach else none for r in near}
        s = {r: [state(k - 1, r, f) for f in range(NF)] for r in near if -reach - 1 <= r < OWN + reach + 1}

        def times(r, l, c):
            return None if lam[r][c] is None else s[r][2 + l] * lam[r][c]

        va = {r: [times(r, l, l) for l in range(2)] for r in near}
        vb = {r: [times(r, l, 2 + l) for l in range(2)] for r in near}
        outs = []
        for r in rows:
            lo, hi = r - 1, r + 1
            new, grads = [None] * NF, [None] * 2
            cor = COR[pl.ds(PAD + r, 1), :]
            for l in range(2):
                u, v, h = s[r][l], s[r][2 + l], s[r][4 + l]
                a, b, c = lam[r][l], lam[r][2 + l], lam[r][4 + l]
                mass = get(B0, PAD + r, 6 + l, BW) + h
                cy = less(lam[hi][4 + l], lam[lo][4 + l])
                ya, yb = less(va[hi][l], va[lo][l]), less(vb[hi][l], vb[lo][l])
                by = less(lam[hi][2 + l], lam[lo][2 + l])
                if a is None:
                    new[l] = HALF_C * ya
                    new[2 + l] = HALF_C * (yb + mass * cy)
                    new[4 + l] = HALF_C * (v * cy)
                    grads[l] = by
                    continue
                cx = along_x(c)
                dxu, dxv = get(DX.at[k - 1], PAD + r, l, 4), get(DX.at[k - 1], PAD + r, 2 + l, 4)
                new[l] = a - cor * b - HALF_C * (a * dxu + b * dxv - along_x(u * a) - ya - mass * cx)
                new[2 + l] = b + cor * a - HALF_C * (
                    a * (s[hi][l] - s[lo][l]) + b * (s[hi][2 + l] - s[lo][2 + l]) - along_x(u * b) - yb - mass * cy)
                new[4 + l] = c + HALF_C * (u * cx + v * cy)
                grads[l] = along_x(a) + by
            new[4] = new[4] + HALF_C * (grads[0] + grads[1])
            new[5] = new[5] + HALF_C * grads[1]
            ok = side_ok(r)
            if k > 1 and ok is None:
                for l in range(2):
                    new[4 + l] = new[4 + l] + pull(k - 1, r, l)
            if ok is not None:
                new = [value * ok for value in new]
            outs.append((r, new))
        for r, new in outs:
            fresh = r == -reach - 1 or r == OWN + reach
            for f in range(NF):
                put(dst, PAD + r, f, new[f])
                if k > 1:
                    put(G, PAD + r, f, new[f] if fresh else get(G, PAD + r, f) + new[f])

    for k in range(STEPS, 0, -1):
        reach = STEPS - k + 1
        half = OWN // 2 + reach
        backward(k, range(-reach, half - reach))
        backward(k, range(half - reach, OWN + reach))

    CH = OWN * RW // win_n

    def chunk(p):
        return pl.ds(pl.multiple_of(PAD * RW + p * CH, SUB), CH)

    g_halo = [
        to_tile(G, (PAD + OWN) * RW, GH.at[0], 0, (PAD - 1) * RW, (h_s, h_r), 1, 0),
        to_tile(G, RW, GH.at[1], 0, (PAD - 1) * RW, (h_s, h_r), 1, 1)]
    start([g_halo])
    arrive([g_halo])

    def add_halo(at, src):
        span = pl.ds(at * RW, (PAD - 1) * RW)
        G[span, :] = G[span, :] + src[...]

    @pl.when(low_tile)
    def _():
        add_halo(PAD, GH.at[0])

    @pl.when(high_tile)
    def _():
        add_halo(PAD + OWN - PAD + 1, GH.at[1])

    for n, (a, b) in enumerate(peers):
        p = peer(a, b)
        pltpu.make_async_remote_copy(
            src_ref=G.at[chunk(p), :], dst_ref=RS.at[pl.ds(n * CH, CH), :], send_sem=rs_s, recv_sem=rs_r,
            device_id={"win": p, "tile": t}, device_id_type=MESH).start()

    lam_halo = [
        to_tile(LAM.at[0], (PAD + OWN) * RW, LH.at[0], 0, PAD * RW, (h_s, h_r), 0, 0),
        to_tile(LAM.at[0], 0, LH.at[1], 0, PAD * RW, (h_s, h_r), 0, 1)]
    start([lam_halo])

    def all_of(ref, count, sem):
        part = ref.at[pl.ds(0, count * CH), :]
        pltpu.make_async_copy(part, part, sem).wait()

    all_of(RS, win_n - 1, rs_r)
    total = G[chunk(w), :]
    for n in range(win_n - 1):
        total = total + RS[pl.ds(n * CH, CH), :]
    RED[...] = total

    mine = pl.ds(pl.multiple_of(w * CH, SUB), CH)
    for a, b in peers:
        pltpu.make_async_remote_copy(
            src_ref=RED, dst_ref=AG.at[mine, :], send_sem=ag_s, recv_sem=ag_r,
            device_id={"win": peer(a, b), "tile": t}, device_id_type=MESH).start()
    AG[mine, :] = RED[...]

    arrive([lam_halo])

    def add_rows(at, src):
        span = pl.ds(at * RW, PAD * RW)
        LAM[0, span, :] = LAM[0, span, :] + src[...]

    @pl.when(low_tile)
    def _():
        add_rows(PAD, LH.at[0])

    @pl.when(high_tile)
    def _():
        add_rows(PAD + OWN - PAD, LH.at[1])

    @pl.when(w > 0)
    def _():
        mu.wait_recv()

    @pl.when(w == 0)
    def _():
        EARL[...] = jnp.zeros_like(EARL)

    def gather(src, first, f, s):
        return src[pl.ds((first * NF + f) * SUB + s, OWN, stride=RW), :]

    for f in range(NF):
        for s in range(SUB):
            gs_out[0, f // 2, f % 2, :, pl.ds(128 * s, 128)] = (
                gather(LAM.at[0], PAD, f, s) + gather(EARL, 0, f, s))

    all_of(AG, win_n - 1, ag_r)
    for f in range(NF):
        for s in range(SUB):
            gf_out[f // 2, f % 2, :, pl.ds(128 * s, 128)] = gather(AG, 0, f, s)

    left(first + [lam_halo, g_halo])

    @pl.when(w > 0)
    def _():
        nxt.wait_send()

    @pl.when(w < win_n - 1)
    def _():
        mu.wait_send()

    all_of(RS, win_n - 1, rs_s)
    all_of(RS, win_n - 1, ag_s)


def solution(mesh):
    win_n, tile_n = mesh.shape["win"], mesh.shape["tile"]

    def local(traj, forc, dep, ostep, oval, owt, ew):
        f32 = jnp.float32

        def flat(rows, width, dtype=f32, lead=()):
            return pltpu.VMEM(lead + (rows * width * SUB, 128), dtype)

        vm = pl.BlockSpec(memory_space=pltpu.VMEM)
        hbm = pl.BlockSpec(memory_space=pl.ANY)
        sem = pltpu.SemaphoreType.DMA
        return pl.pallas_call(
            functools.partial(kernel, win_n, tile_n),
            out_shape=(jax.ShapeDtypeStruct(traj.shape, f32), jax.ShapeDtypeStruct(forc.shape, f32)),
            in_specs=[hbm] * 6 + [pl.BlockSpec(memory_space=pltpu.SMEM)],
            out_specs=(vm, vm),
            scratch_shapes=[
                pltpu.VMEM(traj.shape[1:], f32), pltpu.VMEM(forc.shape, f32), pltpu.VMEM(dep.shape, f32),
                pltpu.VMEM(ostep.shape[1:], jnp.int32), pltpu.VMEM(oval.shape[1:], f32),
                pltpu.VMEM(owt.shape, f32),
                flat(ROWS, BW),
                flat(ROWS, NF, lead=(STEPS,)),
                flat(ROWS, 4, lead=(STEPS,)),
                flat(OWN + 1, 1, jnp.int32),
                flat(OWN + 1, 2),
                flat(OWN + 1, 1),
                pltpu.VMEM((24, 128), f32),
                pltpu.VMEM(traj.shape[1:], f32),
                flat(OWN + 1, NF),
                flat(OWN, NF),
                flat(OWN, NF),
                flat(ROWS, NF, lead=(2,)),
                flat(ROWS, NF),
                flat(PAD - 1, NF, lead=(2,)),
                flat(PAD, NF, lead=(2,)),
                flat(OWN, NF),
                pltpu.VMEM((OWN * RW // win_n, 128), f32),
                flat(OWN, NF),
                sem((6,)), sem((4, 2)), sem((4, 2)), sem, sem, sem, sem, sem((2, 2)), sem((2, 2)),
                sem, sem, sem, sem,
            ],
            compiler_params=pltpu.CompilerParams(
                collective_id=0, has_side_effects=True, vmem_limit_bytes=60 * 2**20),
        )(traj, forc, dep, ostep, oval, owt, ew.T)

    return jax.shard_map(
        local,
        mesh=mesh,
        in_specs=(
            P("win", None, None, "tile", None),
            P(None, None, "tile", None),
            P(None, "tile", None),
            P("win", "tile", None),
            P("win", None, "tile", None),
            P("tile", None),
            P(),
        ),
        out_specs=(P("win", None, None, "tile", None), P(None, None, "tile", None)),
        check_vma=False,
    )
```

```python
import functools

import jax
import jax.numpy as jnp
from jax import lax
from jax.experimental import pallas as pl
from jax.experimental.pallas import tpu as pltpu
from jax.sharding import PartitionSpec as P

MESH = pl.DeviceIdType.MESH
STEPS = 6
LAT_ROWS = 2048
C_STEP = 0.2
HALF_C = 0.1
OWN = 8
PAD = STEPS
ROWS = OWN + 2 * PAD
NF = 6
SUB = 8
RW = NF * SUB
BW = 14
BR = BW * SUB


def along_x(a):
    lane = lax.broadcasted_iota(jnp.int32, a.shape, 1)
    up = pltpu.roll(a, 127, 1)
    up = jnp.where(lane == 127, pltpu.roll(up, SUB - 1, 0), up)
    down = pltpu.roll(a, 1, 1)
    down = jnp.where(lane == 0, pltpu.roll(down, 1, 0), down)
    return up - down


def get(ref, row, f, width=NF):
    return ref[pl.ds((row * width + f) * SUB, SUB), :]


def put(ref, row, f, value, width=NF):
    ref[pl.ds((row * width + f) * SUB, SUB), :] = value


def less(a, b):
    if a is None:
        return None if b is None else -b
    return a if b is None else a - b


def kernel(
    win_n, tile_n, traj, forc, dep, ostep, oval, owt, ew_in,
    gs_out, gf_out,
    TT, TF, TD, TS, TV, TW, ew,
    B0, X, DX, OS, OV, OW, COR, NT, NXT, MU, EARL, LAM, G, GH, LH, RS, RED, AG,
    in_s, init_s, init_r, nxt_s, nxt_r, mu_s, mu_r, h_s, h_r, rs_s, rs_r, ag_s, ag_r,
):
    w = lax.axis_index("win")
    t = lax.axis_index("tile")
    y, x = w // 4, lax.rem(w, 4)
    low_tile, high_tile = t > 0, t < tile_n - 1

    def peer(a, b):
        return lax.rem(y + a, 4) * 4 + lax.rem(x + b, 4)

    peers = [(a, b) for a in range(4) for b in range(4) if a or b]
    peers.sort(key=lambda p: -(min(p[0], 4 - p[0]) + min(p[1], 4 - p[1])))

    ins = [pltpu.make_async_copy(src, dst, in_s.at[n]) for n, (src, dst) in enumerate(
        [(traj.at[0], TT), (dep, TD), (forc, TF), (ostep.at[0], TS), (oval.at[0], TV), (owt, TW), (ew_in, ew)])]
    for c in ins:
        c.start()

    barrier = pltpu.get_barrier_semaphore()

    def greet(win, tile):
        pl.semaphore_signal(barrier, inc=1, device_id={"win": win, "tile": tile}, device_id_type=MESH)

    for a, b in peers:
        greet(peer(a, b), t)

    @pl.when(low_tile)
    def _():
        greet(w, t - 1)

    @pl.when(high_tile)
    def _():
        greet(w, t + 1)

    band_row = lax.broadcasted_iota(jnp.int32, (24, 128), 0) + (t * OWN - PAD)
    lat = ((LAT_ROWS - tile_n * OWN) // 2 + band_row).astype(jnp.float32)
    COR[...] = (2.0 * C_STEP) * jnp.sin(jnp.pi * ((lat + 0.5) / LAT_ROWS - 0.5))
    low_ok = jnp.where(low_tile, 1.0, 0.0)
    high_ok = jnp.where(high_tile, 1.0, 0.0)

    @pl.when(t == 0)
    def _():
        B0[pl.ds(0, PAD * BR), :] = jnp.zeros((PAD * BR, 128), jnp.float32)

    @pl.when(t == tile_n - 1)
    def _():
        B0[pl.ds((PAD + OWN) * BR, PAD * BR), :] = jnp.zeros((PAD * BR, 128), jnp.float32)

    def spread(dst, first, width, f, tile):
        for s in range(SUB):
            dst[pl.ds((first * width + f) * SUB + s, OWN, stride=width * SUB), :] = tile(pl.ds(128 * s, 128))

    ins[0].wait()
    for f in range(NF):
        spread(B0, PAD, BW, f, lambda cols: TT[f // 2, f % 2, :, cols])
    ins[1].wait()
    for l in range(2):
        spread(B0, PAD, BW, 6 + l, lambda cols: TD[l, :, cols])
    ins[2].wait()
    for f in range(NF):
        spread(B0, PAD, BW, 8 + f, lambda cols: TF[f // 2, f % 2, :, cols])

    pl.semaphore_wait(barrier, win_n - 1 + jnp.where(low_tile, 1, 0) + jnp.where(high_tile, 1, 0))

    def to_tile(src, src_at, dst, dst_at, size, sems, n, side):
        return pltpu.make_async_remote_copy(
            src_ref=src.at[pl.ds(src_at, size), :], dst_ref=dst.at[pl.ds(dst_at, size), :],
            send_sem=sems[0].at[n, side], recv_sem=sems[1].at[n, side],
            device_id={"win": w, "tile": t + 1 if side == 0 else t - 1}, device_id_type=MESH)

    def init(n, near, count, size):
        up = (PAD + OWN - near - count + 1) * BR, (PAD - near - count + 1) * BR
        down = (PAD + near - 1) * BR, (PAD + OWN + near - 1) * BR
        return [to_tile(B0, a, B0, b, size, (init_s, init_r), n, side) for side, (a, b) in enumerate((up, down))]

    first = [init(0, 1, 2, 2 * BR), init(1, 3, 2, 2 * BR), init(2, 5, 1, BR), init(3, 6, 1, SUB * SUB)]

    def start(pairs):
        @pl.when(high_tile)
        def _():
            for c in pairs:
                c[0].start()

        @pl.when(low_tile)
        def _():
            for c in pairs:
                c[1].start()

    def arrive(pairs):
        @pl.when(low_tile)
        def _():
            for c in pairs:
                c[0].wait_recv()

        @pl.when(high_tile)
        def _():
            for c in pairs:
                c[1].wait_recv()

    def left(pairs):
        @pl.when(high_tile)
        def _():
            for c in pairs:
                c[0].wait_send()

        @pl.when(low_tile)
        def _():
            for c in pairs:
                c[1].wait_send()

    start(first)
    nxt = pltpu.make_async_remote_copy(
        src_ref=TT, dst_ref=NT, send_sem=nxt_s, recv_sem=nxt_r,
        device_id={"win": w - 1, "tile": t}, device_id_type=MESH)

    @pl.when(w > 0)
    def _():
        nxt.start()

    def state(k, r, f):
        return get(B0, PAD + r, f, BW) if k == 0 else get(X.at[k - 1], PAD + r, f)

    def side_ok(r):
        return low_ok if r < 0 else high_ok if r >= OWN else None

    def forward(k, blocks):
        outs = []
        for block in blocks:
            near = range(block[0] - 1, block[-1] + 2)
            s = {r: [state(k, r, f) for f in range(NF)] for r in near}
            p = {r: (s[r][4], s[r][4] + s[r][5]) for r in near}
            mass = {r: [get(B0, PAD + r, 6 + l, BW) + s[r][4 + l] for l in range(2)] for r in near}
            q = {r: [mass[r][l] * s[r][2 + l] for l in range(2)] for r in near}
            for r in block:
                cor = COR[pl.ds(PAD + r, 1), :]
                new, dx = [None] * NF, [None] * 4
                lo, hi = r - 1, r + 1
                for l in range(2):
                    u, v, h = s[r][l], s[r][2 + l], s[r][4 + l]
                    dx[l], dx[2 + l] = along_x(u), along_x(v)
                    new[l] = u - HALF_C * (u * dx[l] + v * (s[hi][l] - s[lo][l]) + along_x(p[r][l])) + cor * v
                    new[2 + l] = v - HALF_C * (
                        u * dx[2 + l] + v * (s[hi][2 + l] - s[lo][2 + l]) + (p[hi][l] - p[lo][l])) - cor * u
                    new[4 + l] = h - HALF_C * (along_x(mass[r][l] * u) + (q[hi][l] - q[lo][l]))
                ok = side_ok(r)
                for f in range(NF):
                    new[f] = new[f] + get(B0, PAD + r, 8 + f, BW)
                    if ok is not None:
                        new[f] = new[f] * ok
                outs.append((r, new, dx))
        for r, new, dx in outs:
            for f in range(NF):
                put(X.at[k], PAD + r, f, new[f])
            for f in range(4):
                put(DX.at[k], PAD + r, f, dx[f], 4)

    for k in range(3):
        forward(k, [range(1 + k, OWN - 1 - k)])
    for n, near in enumerate((1, 3, 5)):
        arrive([first[n]] if n < 2 else first[2:])
        if n == 0:
            for c in ins[3:]:
                c.wait()
            spread(OS, 0, 1, 0, lambda cols: TS[:, cols])
            spread(OW, 0, 1, 0, lambda cols: TW[:, cols])
            for l in range(2):
                spread(OV, 0, 2, l, lambda cols: TV[l, :, cols])
        for k in range(STEPS):
            low = [r for r in (k - near, k - near + 1) if r < OWN // 2]
            high = [OWN - 1 - r for r in reversed(low)]
            if low:
                forward(k, [low, high])

    not_last = jnp.where(w < win_n - 1, 1.0, 0.0)

    @pl.when(w < win_n - 1)
    def _():
        nxt.wait_recv()

    @pl.when(w == win_n - 1)
    def _():
        NT[...] = jnp.zeros_like(NT)

    for f in range(NF):
        spread(NXT, 0, NF, f, lambda cols: NT[f // 2, f % 2, :, cols])

    def pull(k, r, l):
        ow = jnp.where(get(OS, r, 0, 1) == k, get(OW, r, 0, 1), 0.0)
        return ow * (state(k, r, 4 + l) - get(OV, r, l, 2))

    for r in range(OWN):
        for f in range(NF):
            mis = (ew[f % 2, f // 2] * not_last) * (get(NXT, r, f) - state(STEPS, r, f))
            put(MU, r, f, mis)
            lam = -mis
            if f >= 4:
                lam = lam + pull(STEPS, r, f - 4)
            put(LAM.at[0], PAD + r, f, lam)
            put(G, PAD + r, f, lam)
    mu = pltpu.make_async_remote_copy(
        src_ref=MU, dst_ref=EARL, send_sem=mu_s, recv_sem=mu_r,
        device_id={"win": w + 1, "tile": t}, device_id_type=MESH)

    @pl.when(w < win_n - 1)
    def _():
        mu.start()

    def backward(k, rows):
        src, dst = LAM.at[STEPS - k], LAM.at[STEPS - k + 1]
        reach = STEPS - k
        none = [None] * NF
        near = range(rows[0] - 1, rows[-1] + 2)
        lam = {r: [get(src, PAD + r, f) for f in range(NF)] if -reach <= r < OWN + reach else none for r in near}
        s = {r: [state(k - 1, r, f) for f in range(NF)] for r in near if -reach - 1 <= r < OWN + reach + 1}

        def times(r, l, c):
            return None if lam[r][c] is None else s[r][2 + l] * lam[r][c]

        va = {r: [times(r, l, l) for l in range(2)] for r in near}
        vb = {r: [times(r, l, 2 + l) for l in range(2)] for r in near}
        outs = []
        for r in rows:
            lo, hi = r - 1, r + 1
            new, grads = [None] * NF, [None] * 2
            cor = COR[pl.ds(PAD + r, 1), :]
            for l in range(2):
                u, v, h = s[r][l], s[r][2 + l], s[r][4 + l]
                a, b, c = lam[r][l], lam[r][2 + l], lam[r][4 + l]
                mass = get(B0, PAD + r, 6 + l, BW) + h
                cy = less(lam[hi][4 + l], lam[lo][4 + l])
                ya, yb = less(va[hi][l], va[lo][l]), less(vb[hi][l], vb[lo][l])
                by = less(lam[hi][2 + l], lam[lo][2 + l])
                if a is None:
                    new[l] = HALF_C * ya
                    new[2 + l] = HALF_C * (yb + mass * cy)
                    new[4 + l] = HALF_C * (v * cy)
                    grads[l] = by
                    continue
                cx = along_x(c)
                dxu, dxv = get(DX.at[k - 1], PAD + r, l, 4), get(DX.at[k - 1], PAD + r, 2 + l, 4)
                new[l] = a - cor * b - HALF_C * (a * dxu + b * dxv - along_x(u * a) - ya - mass * cx)
                new[2 + l] = b + cor * a - HALF_C * (
                    a * (s[hi][l] - s[lo][l]) + b * (s[hi][2 + l] - s[lo][2 + l]) - along_x(u * b) - yb - mass * cy)
                new[4 + l] = c + HALF_C * (u * cx + v * cy)
                grads[l] = along_x(a) + by
            new[4] = new[4] + HALF_C * (grads[0] + grads[1])
            new[5] = new[5] + HALF_C * grads[1]
            ok = side_ok(r)
            if k > 1 and ok is None:
                for l in range(2):
                    new[4 + l] = new[4 + l] + pull(k - 1, r, l)
            if ok is not None:
                new = [value * ok for value in new]
            outs.append((r, new))
        for r, new in outs:
            fresh = r == -reach - 1 or r == OWN + reach
            for f in range(NF):
                put(dst, PAD + r, f, new[f])
                if k > 1:
                    put(G, PAD + r, f, new[f] if fresh else get(G, PAD + r, f) + new[f])

    backward(STEPS, range(-1, OWN + 1))
    for k in range(STEPS - 1, 1, -1):
        reach = STEPS - k + 1
        backward(k, range(-reach, k - 2))
        backward(k, range(OWN + 2 - k, OWN + reach))
    g_halo = [
        to_tile(G, (PAD + OWN) * RW, GH.at[0], 0, (PAD - 1) * RW, (h_s, h_r), 1, 0),
        to_tile(G, RW, GH.at[1], 0, (PAD - 1) * RW, (h_s, h_r), 1, 1)]
    start([g_halo])
    for k in range(STEPS - 1, 1, -1):
        backward(k, range(k - 2, OWN + 2 - k))
    backward(1, range(-STEPS, OWN // 2))
    backward(1, range(OWN // 2, OWN + STEPS))
    last = LAM.at[STEPS]
    lam_halo = [
        to_tile(last, (PAD + OWN) * RW, LH.at[0], 0, PAD * RW, (h_s, h_r), 0, 0),
        to_tile(last, 0, LH.at[1], 0, PAD * RW, (h_s, h_r), 0, 1)]
    start([lam_halo])

    CH = OWN * RW // win_n

    def chunk(p):
        return pl.ds(pl.multiple_of(PAD * RW + p * CH, SUB), CH)

    arrive([g_halo])

    def add_halo(at, src):
        span = pl.ds(at * RW, (PAD - 1) * RW)
        G[span, :] = G[span, :] + src[...]

    @pl.when(low_tile)
    def _():
        add_halo(PAD, GH.at[0])

    @pl.when(high_tile)
    def _():
        add_halo(PAD + OWN - PAD + 1, GH.at[1])

    for n, (a, b) in enumerate(peers):
        p = peer(a, b)
        pltpu.make_async_remote_copy(
            src_ref=G.at[chunk(p), :], dst_ref=RS.at[pl.ds(n * CH, CH), :], send_sem=rs_s, recv_sem=rs_r,
            device_id={"win": p, "tile": t}, device_id_type=MESH).start()

    def all_of(ref, count, sem):
        part = ref.at[pl.ds(0, count * CH), :]
        pltpu.make_async_copy(part, part, sem).wait()

    all_of(RS, win_n - 1, rs_r)
    total = G[chunk(w), :]
    for n in range(win_n - 1):
        total = total + RS[pl.ds(n * CH, CH), :]
    RED[...] = total

    mine = pl.ds(pl.multiple_of(w * CH, SUB), CH)
    for a, b in peers:
        pltpu.make_async_remote_copy(
            src_ref=RED, dst_ref=AG.at[mine, :], send_sem=ag_s, recv_sem=ag_r,
            device_id={"win": peer(a, b), "tile": t}, device_id_type=MESH).start()
    AG[mine, :] = RED[...]

    arrive([lam_halo])

    def add_rows(at, src):
        span = pl.ds(at * RW, PAD * RW)
        last[span, :] = last[span, :] + src[...]

    @pl.when(low_tile)
    def _():
        add_rows(PAD, LH.at[0])

    @pl.when(high_tile)
    def _():
        add_rows(PAD + OWN - PAD, LH.at[1])

    @pl.when(w > 0)
    def _():
        mu.wait_recv()

    @pl.when(w == 0)
    def _():
        EARL[...] = jnp.zeros_like(EARL)

    def gather(src, first, f, s):
        return src[pl.ds((first * NF + f) * SUB + s, OWN, stride=RW), :]

    for f in range(NF):
        for s in range(SUB):
            gs_out[0, f // 2, f % 2, :, pl.ds(128 * s, 128)] = (
                gather(last, PAD, f, s) + gather(EARL, 0, f, s))

    all_of(AG, win_n - 1, ag_r)
    for f in range(NF):
        for s in range(SUB):
            gf_out[f // 2, f % 2, :, pl.ds(128 * s, 128)] = gather(AG, 0, f, s)

    left(first + [lam_halo, g_halo])

    @pl.when(w > 0)
    def _():
        nxt.wait_send()

    @pl.when(w < win_n - 1)
    def _():
        mu.wait_send()

    all_of(RS, win_n - 1, rs_s)
    all_of(RS, win_n - 1, ag_s)


def hand_over(a, b, a_out, b_out, sems):
    copies = [pltpu.make_async_copy(src, dst, sems.at[n]) for n, (src, dst) in enumerate([(a, a_out), (b, b_out)])]
    for c in copies:
        c.start()
    for c in copies:
        c.wait()


def solution(mesh):
    win_n, tile_n = mesh.shape["win"], mesh.shape["tile"]

    def local(traj, forc, dep, ostep, oval, owt, ew):
        f32 = jnp.float32

        def flat(rows, width, dtype=f32, lead=()):
            return pltpu.VMEM(lead + (rows * width * SUB, 128), dtype)

        vm = pl.BlockSpec(memory_space=pltpu.VMEM)
        hbm = pl.BlockSpec(memory_space=pltpu.HBM)
        sem = pltpu.SemaphoreType.DMA
        results = pl.pallas_call(
            functools.partial(kernel, win_n, tile_n),
            out_shape=(jax.ShapeDtypeStruct(traj.shape, f32), jax.ShapeDtypeStruct(forc.shape, f32)),
            in_specs=[hbm] * 7,
            out_specs=(vm, vm),
            scratch_shapes=[
                pltpu.VMEM(traj.shape[1:], f32), pltpu.VMEM(forc.shape, f32), pltpu.VMEM(dep.shape, f32),
                pltpu.VMEM(ostep.shape[1:], jnp.int32), pltpu.VMEM(oval.shape[1:], f32),
                pltpu.VMEM(owt.shape, f32), pltpu.SMEM((2, 3), f32),
                flat(ROWS, BW),
                flat(ROWS, NF, lead=(STEPS,)),
                flat(ROWS, 4, lead=(STEPS,)),
                flat(OWN + 1, 1, jnp.int32),
                flat(OWN + 1, 2),
                flat(OWN + 1, 1),
                pltpu.VMEM((24, 128), f32),
                pltpu.VMEM(traj.shape[1:], f32),
                flat(OWN + 1, NF),
                flat(OWN, NF),
                flat(OWN, NF),
                flat(ROWS, NF, lead=(STEPS + 1,)),
                flat(ROWS, NF),
                flat(PAD - 1, NF, lead=(2,)),
                flat(PAD, NF, lead=(2,)),
                flat(OWN, NF),
                pltpu.VMEM((OWN * RW // win_n, 128), f32),
                flat(OWN, NF),
                sem((7,)), sem((4, 2)), sem((4, 2)), sem, sem, sem, sem, sem((2, 2)), sem((2, 2)),
                sem, sem, sem, sem,
            ],
            compiler_params=pltpu.CompilerParams(
                collective_id=0, has_side_effects=True, vmem_limit_bytes=16 * 2**20),
        )(*[pltpu.with_memory_space_constraint(z, pltpu.HBM) for z in (traj, forc, dep, ostep, oval, owt, ew.T)])
        out = pl.BlockSpec(memory_space=pl.ANY)
        return pl.pallas_call(
            hand_over,
            out_shape=[jax.ShapeDtypeStruct(r.shape, f32) for r in results],
            in_specs=[out] * 2,
            out_specs=[out] * 2,
            scratch_shapes=[sem((2,))],
        )(*results)

    return jax.shard_map(
        local,
        mesh=mesh,
        in_specs=(
            P("win", None, None, "tile", None),
            P(None, None, "tile", None),
            P(None, "tile", None),
            P("win", "tile", None),
            P("win", None, "tile", None),
            P("tile", None),
            P(),
        ),
        out_specs=(P("win", None, None, "tile", None), P(None, None, "tile", None)),
        check_vma=False,
    )
```

```python
import functools

import jax
import jax.numpy as jnp
from jax import lax
from jax.experimental import pallas as pl
from jax.experimental.pallas import tpu as pltpu
from jax.sharding import PartitionSpec as P

MESH = pl.DeviceIdType.MESH
STEPS = 6
LAT_ROWS = 2048
C_STEP = 0.2
HALF_C = 0.1
OWN = 8
PAD = STEPS
ROWS = OWN + 2 * PAD
NF = 6
SUB = 8
RW = NF * SUB
BW = 14
BR = BW * SUB


def along_x(a):
    lane = lax.broadcasted_iota(jnp.int32, a.shape, 1)
    up = pltpu.roll(a, 127, 1)
    up = jnp.where(lane == 127, pltpu.roll(up, SUB - 1, 0), up)
    down = pltpu.roll(a, 1, 1)
    down = jnp.where(lane == 0, pltpu.roll(down, 1, 0), down)
    return up - down


def get(ref, row, f, width=NF):
    return ref[pl.ds((row * width + f) * SUB, SUB), :]


def put(ref, row, f, value, width=NF):
    ref[pl.ds((row * width + f) * SUB, SUB), :] = value


def less(a, b):
    if a is None:
        return None if b is None else -b
    return a if b is None else a - b


def kernel(
    win_n, tile_n, traj, forc, dep, ostep, oval, owt, ew_in,
    gs_out, gf_out,
    TT, TF, TD, TS, TV, TW, ew,
    B0, X, DX, OS, OV, OW, COR, NT, NXT, MU, EARL, LAM, G, GH, LH, RS, RED, AG,
    in_s, init_s, init_r, nxt_s, nxt_r, mu_s, mu_r, h_s, h_r, rs_s, rs_r, ag_s, ag_r,
):
    w = lax.axis_index("win")
    t = lax.axis_index("tile")
    y, x = w // 4, lax.rem(w, 4)
    low_tile, high_tile = t > 0, t < tile_n - 1

    def peer(a, b):
        return lax.rem(y + a, 4) * 4 + lax.rem(x + b, 4)

    peers = [(a, b) for a in range(4) for b in range(4) if a or b]
    peers.sort(key=lambda p: -(min(p[0], 4 - p[0]) + min(p[1], 4 - p[1])))

    ins = [pltpu.make_async_copy(src, dst, in_s.at[n]) for n, (src, dst) in enumerate(
        [(traj.at[0], TT), (dep, TD), (forc, TF), (ostep.at[0], TS), (oval.at[0], TV), (owt, TW), (ew_in, ew)])]
    for c in ins:
        c.start()

    barrier = pltpu.get_barrier_semaphore()

    def greet(win, tile):
        pl.semaphore_signal(barrier, inc=1, device_id={"win": win, "tile": tile}, device_id_type=MESH)

    for a, b in peers:
        greet(peer(a, b), t)

    @pl.when(low_tile)
    def _():
        greet(w, t - 1)

    @pl.when(high_tile)
    def _():
        greet(w, t + 1)

    band_row = lax.broadcasted_iota(jnp.int32, (24, 128), 0) + (t * OWN - PAD)
    lat = ((LAT_ROWS - tile_n * OWN) // 2 + band_row).astype(jnp.float32)
    COR[...] = (2.0 * C_STEP) * jnp.sin(jnp.pi * ((lat + 0.5) / LAT_ROWS - 0.5))
    low_ok = jnp.where(low_tile, 1.0, 0.0)
    high_ok = jnp.where(high_tile, 1.0, 0.0)

    @pl.when(t == 0)
    def _():
        B0[pl.ds(0, PAD * BR), :] = jnp.zeros((PAD * BR, 128), jnp.float32)

    @pl.when(t == tile_n - 1)
    def _():
        B0[pl.ds((PAD + OWN) * BR, PAD * BR), :] = jnp.zeros((PAD * BR, 128), jnp.float32)

    def spread(dst, first, width, f, tile):
        for s in range(SUB):
            dst[pl.ds((first * width + f) * SUB + s, OWN, stride=width * SUB), :] = tile(pl.ds(128 * s, 128))

    ins[0].wait()
    for f in range(NF):
        spread(B0, PAD, BW, f, lambda cols: TT[f // 2, f % 2, :, cols])
    ins[1].wait()
    for l in range(2):
        spread(B0, PAD, BW, 6 + l, lambda cols: TD[l, :, cols])
    ins[2].wait()
    for f in range(NF):
        spread(B0, PAD, BW, 8 + f, lambda cols: TF[f // 2, f % 2, :, cols])

    pl.semaphore_wait(barrier, win_n - 1 + jnp.where(low_tile, 1, 0) + jnp.where(high_tile, 1, 0))

    def to_tile(src, src_at, dst, dst_at, size, sems, n, side):
        return pltpu.make_async_remote_copy(
            src_ref=src.at[pl.ds(src_at, size), :], dst_ref=dst.at[pl.ds(dst_at, size), :],
            send_sem=sems[0].at[n, side], recv_sem=sems[1].at[n, side],
            device_id={"win": w, "tile": t + 1 if side == 0 else t - 1}, device_id_type=MESH)

    def init(n, near, count, size):
        up = (PAD + OWN - near - count + 1) * BR, (PAD - near - count + 1) * BR
        down = (PAD + near - 1) * BR, (PAD + OWN + near - 1) * BR
        return [to_tile(B0, a, B0, b, size, (init_s, init_r), n, side) for side, (a, b) in enumerate((up, down))]

    first = [init(0, 1, 2, 2 * BR), init(1, 3, 2, 2 * BR), init(2, 5, 1, BR), init(3, 6, 1, SUB * SUB)]

    def start(pairs):
        @pl.when(high_tile)
        def _():
            for c in pairs:
                c[0].start()

        @pl.when(low_tile)
        def _():
            for c in pairs:
                c[1].start()

    def arrive(pairs):
        @pl.when(low_tile)
        def _():
            for c in pairs:
                c[0].wait_recv()

        @pl.when(high_tile)
        def _():
            for c in pairs:
                c[1].wait_recv()

    def left(pairs):
        @pl.when(high_tile)
        def _():
            for c in pairs:
                c[0].wait_send()

        @pl.when(low_tile)
        def _():
            for c in pairs:
                c[1].wait_send()

    start(first)
    nxt = pltpu.make_async_remote_copy(
        src_ref=TT, dst_ref=NT, send_sem=nxt_s, recv_sem=nxt_r,
        device_id={"win": w - 1, "tile": t}, device_id_type=MESH)

    @pl.when(w > 0)
    def _():
        nxt.start()

    def state(k, r, f):
        return get(B0, PAD + r, f, BW) if k == 0 else get(X.at[k - 1], PAD + r, f)

    def side_ok(r):
        return low_ok if r < 0 else high_ok if r >= OWN else None

    def forward(k, blocks):
        outs = []
        for block in blocks:
            near = range(block[0] - 1, block[-1] + 2)
            s = {r: [state(k, r, f) for f in range(NF)] for r in near}
            p = {r: (s[r][4], s[r][4] + s[r][5]) for r in near}
            mass = {r: [get(B0, PAD + r, 6 + l, BW) + s[r][4 + l] for l in range(2)] for r in near}
            q = {r: [mass[r][l] * s[r][2 + l] for l in range(2)] for r in near}
            for r in block:
                cor = COR[pl.ds(PAD + r, 1), :]
                new, dx = [None] * NF, [None] * 4
                lo, hi = r - 1, r + 1
                for l in range(2):
                    u, v, h = s[r][l], s[r][2 + l], s[r][4 + l]
                    dx[l], dx[2 + l] = along_x(u), along_x(v)
                    new[l] = u - HALF_C * (u * dx[l] + v * (s[hi][l] - s[lo][l]) + along_x(p[r][l])) + cor * v
                    new[2 + l] = v - HALF_C * (
                        u * dx[2 + l] + v * (s[hi][2 + l] - s[lo][2 + l]) + (p[hi][l] - p[lo][l])) - cor * u
                    new[4 + l] = h - HALF_C * (along_x(mass[r][l] * u) + (q[hi][l] - q[lo][l]))
                ok = side_ok(r)
                for f in range(NF):
                    new[f] = new[f] + get(B0, PAD + r, 8 + f, BW)
                    if ok is not None:
                        new[f] = new[f] * ok
                outs.append((r, new, dx))
        for r, new, dx in outs:
            for f in range(NF):
                put(X.at[k], PAD + r, f, new[f])
            for f in range(4):
                put(DX.at[k], PAD + r, f, dx[f], 4)

    for k in range(3):
        forward(k, [range(1 + k, OWN - 1 - k)])
    for n, near in enumerate((1, 3, 5)):
        arrive([first[n]] if n < 2 else first[2:])
        if n == 0:
            for c in ins[3:]:
                c.wait()
            spread(OS, 0, 1, 0, lambda cols: TS[:, cols])
            spread(OW, 0, 1, 0, lambda cols: TW[:, cols])
            for l in range(2):
                spread(OV, 0, 2, l, lambda cols: TV[l, :, cols])
        for k in range(STEPS):
            low = [r for r in (k - near, k - near + 1) if r < OWN // 2]
            high = [OWN - 1 - r for r in reversed(low)]
            if low:
                forward(k, [low, high])

    not_last = jnp.where(w < win_n - 1, 1.0, 0.0)

    @pl.when(w < win_n - 1)
    def _():
        nxt.wait_recv()

    @pl.when(w == win_n - 1)
    def _():
        NT[...] = jnp.zeros_like(NT)

    for f in range(NF):
        spread(NXT, 0, NF, f, lambda cols: NT[f // 2, f % 2, :, cols])

    def pull(k, r, l):
        ow = jnp.where(get(OS, r, 0, 1) == k, get(OW, r, 0, 1), 0.0)
        return ow * (state(k, r, 4 + l) - get(OV, r, l, 2))

    for r in range(OWN):
        for f in range(NF):
            mis = (ew[f % 2, f // 2] * not_last) * (get(NXT, r, f) - state(STEPS, r, f))
            put(MU, r, f, mis)
            lam = -mis
            if f >= 4:
                lam = lam + pull(STEPS, r, f - 4)
            put(LAM.at[0], PAD + r, f, lam)
            put(G, PAD + r, f, lam)
    mu = pltpu.make_async_remote_copy(
        src_ref=MU, dst_ref=EARL, send_sem=mu_s, recv_sem=mu_r,
        device_id={"win": w + 1, "tile": t}, device_id_type=MESH)

    @pl.when(w < win_n - 1)
    def _():
        mu.start()

    def backward(k, rows):
        src, dst = LAM.at[STEPS - k], LAM.at[STEPS - k + 1]
        reach = STEPS - k
        none = [None] * NF
        near = range(rows[0] - 1, rows[-1] + 2)
        lam = {r: [get(src, PAD + r, f) for f in range(NF)] if -reach <= r < OWN + reach else none for r in near}
        s = {r: [state(k - 1, r, f) for f in range(NF)] for r in near if -reach - 1 <= r < OWN + reach + 1}

        def times(r, l, c):
            return None if lam[r][c] is None else s[r][2 + l] * lam[r][c]

        va = {r: [times(r, l, l) for l in range(2)] for r in near}
        vb = {r: [times(r, l, 2 + l) for l in range(2)] for r in near}
        outs = []
        for r in rows:
            lo, hi = r - 1, r + 1
            new, grads = [None] * NF, [None] * 2
            cor = COR[pl.ds(PAD + r, 1), :]
            for l in range(2):
                u, v, h = s[r][l], s[r][2 + l], s[r][4 + l]
                a, b, c = lam[r][l], lam[r][2 + l], lam[r][4 + l]
                mass = get(B0, PAD + r, 6 + l, BW) + h
                cy = less(lam[hi][4 + l], lam[lo][4 + l])
                ya, yb = less(va[hi][l], va[lo][l]), less(vb[hi][l], vb[lo][l])
                by = less(lam[hi][2 + l], lam[lo][2 + l])
                if a is None:
                    new[l] = HALF_C * ya
                    new[2 + l] = HALF_C * (yb + mass * cy)
                    new[4 + l] = HALF_C * (v * cy)
                    grads[l] = by
                    continue
                cx = along_x(c)
                dxu, dxv = get(DX.at[k - 1], PAD + r, l, 4), get(DX.at[k - 1], PAD + r, 2 + l, 4)
                new[l] = a - cor * b - HALF_C * (a * dxu + b * dxv - along_x(u * a) - ya - mass * cx)
                new[2 + l] = b + cor * a - HALF_C * (
                    a * (s[hi][l] - s[lo][l]) + b * (s[hi][2 + l] - s[lo][2 + l]) - along_x(u * b) - yb - mass * cy)
                new[4 + l] = c + HALF_C * (u * cx + v * cy)
                grads[l] = along_x(a) + by
            new[4] = new[4] + HALF_C * (grads[0] + grads[1])
            new[5] = new[5] + HALF_C * grads[1]
            ok = side_ok(r)
            if k > 1 and ok is None:
                for l in range(2):
                    new[4 + l] = new[4 + l] + pull(k - 1, r, l)
            if ok is not None:
                new = [value * ok for value in new]
            outs.append((r, new))
        for r, new in outs:
            fresh = r == -reach - 1 or r == OWN + reach
            for f in range(NF):
                put(dst, PAD + r, f, new[f])
                if k > 1:
                    put(G, PAD + r, f, new[f] if fresh else get(G, PAD + r, f) + new[f])

    backward(STEPS, range(-1, OWN + 1))
    for k in range(STEPS - 1, 1, -1):
        reach = STEPS - k + 1
        backward(k, range(-reach, k - 2))
        backward(k, range(OWN + 2 - k, OWN + reach))
    g_halo = [
        to_tile(G, (PAD + OWN) * RW, GH.at[0], 0, (PAD - 1) * RW, (h_s, h_r), 1, 0),
        to_tile(G, RW, GH.at[1], 0, (PAD - 1) * RW, (h_s, h_r), 1, 1)]
    start([g_halo])
    for k in range(STEPS - 1, 1, -1):
        backward(k, range(k - 2, OWN + 2 - k))
    backward(1, range(-STEPS, OWN // 2))
    backward(1, range(OWN // 2, OWN + STEPS))
    last = LAM.at[STEPS]
    lam_halo = [
        to_tile(last, (PAD + OWN) * RW, LH.at[0], 0, PAD * RW, (h_s, h_r), 0, 0),
        to_tile(last, 0, LH.at[1], 0, PAD * RW, (h_s, h_r), 0, 1)]
    start([lam_halo])

    CH = OWN * RW // win_n

    def chunk(p):
        return pl.ds(pl.multiple_of(PAD * RW + p * CH, SUB), CH)

    arrive([g_halo])

    def add_halo(at, src):
        span = pl.ds(at * RW, (PAD - 1) * RW)
        G[span, :] = G[span, :] + src[...]

    @pl.when(low_tile)
    def _():
        add_halo(PAD, GH.at[0])

    @pl.when(high_tile)
    def _():
        add_halo(PAD + OWN - PAD + 1, GH.at[1])

    for n, (a, b) in enumerate(peers):
        p = peer(a, b)
        pltpu.make_async_remote_copy(
            src_ref=G.at[chunk(p), :], dst_ref=RS.at[pl.ds(n * CH, CH), :], send_sem=rs_s, recv_sem=rs_r,
            device_id={"win": p, "tile": t}, device_id_type=MESH).start()

    def all_of(ref, count, sem):
        part = ref.at[pl.ds(0, count * CH), :]
        pltpu.make_async_copy(part, part, sem).wait()

    all_of(RS, win_n - 1, rs_r)
    total = G[chunk(w), :]
    for n in range(win_n - 1):
        total = total + RS[pl.ds(n * CH, CH), :]
    RED[...] = total

    mine = pl.ds(pl.multiple_of(w * CH, SUB), CH)
    for a, b in peers:
        pltpu.make_async_remote_copy(
            src_ref=RED, dst_ref=AG.at[mine, :], send_sem=ag_s, recv_sem=ag_r,
            device_id={"win": peer(a, b), "tile": t}, device_id_type=MESH).start()
    AG[mine, :] = RED[...]

    arrive([lam_halo])

    def add_rows(at, src):
        span = pl.ds(at * RW, PAD * RW)
        last[span, :] = last[span, :] + src[...]

    @pl.when(low_tile)
    def _():
        add_rows(PAD, LH.at[0])

    @pl.when(high_tile)
    def _():
        add_rows(PAD + OWN - PAD, LH.at[1])

    @pl.when(w > 0)
    def _():
        mu.wait_recv()

    @pl.when(w == 0)
    def _():
        EARL[...] = jnp.zeros_like(EARL)

    def gather(src, first, f, s):
        return src[pl.ds((first * NF + f) * SUB + s, OWN, stride=RW), :]

    for f in range(NF):
        for s in range(SUB):
            gs_out[0, f // 2, f % 2, :, pl.ds(128 * s, 128)] = (
                gather(last, PAD, f, s) + gather(EARL, 0, f, s))

    all_of(AG, win_n - 1, ag_r)
    for f in range(NF):
        for s in range(SUB):
            gf_out[f // 2, f % 2, :, pl.ds(128 * s, 128)] = gather(AG, 0, f, s)

    left(first + [lam_halo, g_halo])

    @pl.when(w > 0)
    def _():
        nxt.wait_send()

    @pl.when(w < win_n - 1)
    def _():
        mu.wait_send()

    all_of(RS, win_n - 1, rs_s)
    all_of(RS, win_n - 1, ag_s)


def solution(mesh):
    win_n, tile_n = mesh.shape["win"], mesh.shape["tile"]

    def local(traj, forc, dep, ostep, oval, owt, ew):
        f32 = jnp.float32

        def flat(rows, width, dtype=f32, lead=()):
            return pltpu.VMEM(lead + (rows * width * SUB, 128), dtype)

        vm = pl.BlockSpec(memory_space=pltpu.VMEM)
        hbm = pl.BlockSpec(memory_space=pltpu.HBM)
        sem = pltpu.SemaphoreType.DMA
        return pl.pallas_call(
            functools.partial(kernel, win_n, tile_n),
            out_shape=(jax.ShapeDtypeStruct(traj.shape, f32), jax.ShapeDtypeStruct(forc.shape, f32)),
            in_specs=[hbm] * 7,
            out_specs=(vm, vm),
            scratch_shapes=[
                pltpu.VMEM(traj.shape[1:], f32), pltpu.VMEM(forc.shape, f32), pltpu.VMEM(dep.shape, f32),
                pltpu.VMEM(ostep.shape[1:], jnp.int32), pltpu.VMEM(oval.shape[1:], f32),
                pltpu.VMEM(owt.shape, f32), pltpu.SMEM((2, 3), f32),
                flat(ROWS, BW),
                flat(ROWS, NF, lead=(STEPS,)),
                flat(ROWS, 4, lead=(STEPS,)),
                flat(OWN + 1, 1, jnp.int32),
                flat(OWN + 1, 2),
                flat(OWN + 1, 1),
                pltpu.VMEM((24, 128), f32),
                pltpu.VMEM(traj.shape[1:], f32),
                flat(OWN + 1, NF),
                flat(OWN, NF),
                flat(OWN, NF),
                flat(ROWS, NF, lead=(STEPS + 1,)),
                flat(ROWS, NF),
                flat(PAD - 1, NF, lead=(2,)),
                flat(PAD, NF, lead=(2,)),
                flat(OWN, NF),
                pltpu.VMEM((OWN * RW // win_n, 128), f32),
                flat(OWN, NF),
                sem((7,)), sem((4, 2)), sem((4, 2)), sem, sem, sem, sem, sem((2, 2)), sem((2, 2)),
                sem, sem, sem, sem,
            ],
            compiler_params=pltpu.CompilerParams(
                collective_id=0, has_side_effects=True, vmem_limit_bytes=16 * 2**20),
        )(*[pltpu.with_memory_space_constraint(z, pltpu.HBM) for z in (traj, forc, dep, ostep, oval, owt, ew.T)])

    return jax.shard_map(
        local,
        mesh=mesh,
        in_specs=(
            P("win", None, None, "tile", None),
            P(None, None, "tile", None),
            P(None, "tile", None),
            P("win", "tile", None),
            P("win", None, "tile", None),
            P("tile", None),
            P(),
        ),
        out_specs=(P("win", None, None, "tile", None), P(None, None, "tile", None)),
        check_vma=False,
    )
```

```python
import functools

import jax
import jax.numpy as jnp
from jax import lax
from jax.experimental import pallas as pl
from jax.experimental.pallas import tpu as pltpu
from jax.sharding import PartitionSpec as P

MESH = pl.DeviceIdType.MESH
STEPS = 6
LAT_ROWS = 2048
C_STEP = 0.2
HALF_C = 0.1
OWN = 8
PAD = STEPS
ROWS = OWN + 2 * PAD
GP = OWN
NF = 6
SUB = 8
RW = NF * SUB
BW = 14
BR = BW * SUB


def along_x(a):
    lane = lax.broadcasted_iota(jnp.int32, a.shape, 1)
    up = pltpu.roll(a, 127, 1)
    up = jnp.where(lane == 127, pltpu.roll(up, SUB - 1, 0), up)
    down = pltpu.roll(a, 1, 1)
    down = jnp.where(lane == 0, pltpu.roll(down, 1, 0), down)
    return up - down


def get(ref, row, f, width=NF):
    return ref[pl.ds((row * width + f) * SUB, SUB), :]


def put(ref, row, f, value, width=NF):
    ref[pl.ds((row * width + f) * SUB, SUB), :] = value


def less(a, b):
    if a is None:
        return None if b is None else -b
    return a if b is None else a - b


def kernel(
    win_n, tile_n, traj, forc, dep, ostep, oval, owt, ew_in,
    gs_out, gf_out,
    TT, TF, TD, TS, TV, TW, ew,
    B0, X, DX, OS, OV, OW, COR, NT, NXT, MU, EARL, LAM, G, LH, RS, RED, AG,
    in_s, init_s, init_r, nxt_s, nxt_r, mu_s, mu_r, h_s, h_r, rs_s0, rs_s1, rs_s2, rs_r0, rs_r1, rs_r2, ag_s, ag_r,
):
    rs_s, rs_r = (rs_s0, rs_s1, rs_s2), (rs_r0, rs_r1, rs_r2)
    w = lax.axis_index("win")
    t = lax.axis_index("tile")
    y, x = w // 4, lax.rem(w, 4)
    low_tile, high_tile = t > 0, t < tile_n - 1

    def peer(a, b):
        return lax.rem(y + a, 4) * 4 + lax.rem(x + b, 4)

    peers = [(a, b) for a in range(4) for b in range(4) if a or b]
    peers.sort(key=lambda p: -(min(p[0], 4 - p[0]) + min(p[1], 4 - p[1])))

    barrier = pltpu.get_barrier_semaphore()

    def greet(win, tile):
        pl.semaphore_signal(barrier, inc=1, device_id={"win": win, "tile": tile}, device_id_type=MESH)

    @pl.when(low_tile)
    def _():
        greet(w, t - 1)

    @pl.when(high_tile)
    def _():
        greet(w, t + 1)

    ins = [pltpu.make_async_copy(src, dst, in_s.at[n]) for n, (src, dst) in enumerate(
        [(traj.at[0], TT), (dep, TD), (forc, TF), (ostep.at[0], TS), (oval.at[0], TV), (owt, TW), (ew_in, ew)])]
    for c in ins:
        c.start()

    for a, b in peers:
        greet(peer(a, b), t)

    @pl.when(low_tile)
    def _():
        for a, b in peers:
            greet(peer(a, b), t - 1)

    @pl.when(high_tile)
    def _():
        for a, b in peers:
            greet(peer(a, b), t + 1)

    band_row = lax.broadcasted_iota(jnp.int32, (24, 128), 0) + (t * OWN - PAD)
    lat = ((LAT_ROWS - tile_n * OWN) // 2 + band_row).astype(jnp.float32)
    COR[...] = (2.0 * C_STEP) * jnp.sin(jnp.pi * ((lat + 0.5) / LAT_ROWS - 0.5))
    low_ok = jnp.where(low_tile, 1.0, 0.0)
    high_ok = jnp.where(high_tile, 1.0, 0.0)

    @pl.when(t == 0)
    def _():
        B0[pl.ds(0, PAD * BR), :] = jnp.zeros((PAD * BR, 128), jnp.float32)

    @pl.when(t == tile_n - 1)
    def _():
        B0[pl.ds((PAD + OWN) * BR, PAD * BR), :] = jnp.zeros((PAD * BR, 128), jnp.float32)

    def spread(dst, first, width, f, tile):
        for s in range(SUB):
            dst[pl.ds((first * width + f) * SUB + s, OWN, stride=width * SUB), :] = tile(pl.ds(128 * s, 128))

    ins[0].wait()
    for f in range(NF):
        spread(B0, PAD, BW, f, lambda cols: TT[f // 2, f % 2, :, cols])
    ins[1].wait()
    for l in range(2):
        spread(B0, PAD, BW, 6 + l, lambda cols: TD[l, :, cols])
    ins[2].wait()
    for f in range(NF):
        spread(B0, PAD, BW, 8 + f, lambda cols: TF[f // 2, f % 2, :, cols])

    pl.semaphore_wait(barrier, win_n - 1 + jnp.where(low_tile, win_n, 0) + jnp.where(high_tile, win_n, 0))

    def to_tile(src, src_at, dst, dst_at, size, sems, n, side):
        return pltpu.make_async_remote_copy(
            src_ref=src.at[pl.ds(src_at, size), :], dst_ref=dst.at[pl.ds(dst_at, size), :],
            send_sem=sems[0].at[n, side], recv_sem=sems[1].at[n, side],
            device_id={"win": w, "tile": t + 1 if side == 0 else t - 1}, device_id_type=MESH)

    def init(n, near, count, size):
        up = (PAD + OWN - near - count + 1) * BR, (PAD - near - count + 1) * BR
        down = (PAD + near - 1) * BR, (PAD + OWN + near - 1) * BR
        return [to_tile(B0, a, B0, b, size, (init_s, init_r), n, side) for side, (a, b) in enumerate((up, down))]

    first = [init(0, 1, 2, 2 * BR), init(1, 3, 2, 2 * BR), init(2, 5, 1, BR), init(3, 6, 1, SUB * SUB)]

    def start(pairs):
        @pl.when(high_tile)
        def _():
            for c in pairs:
                c[0].start()

        @pl.when(low_tile)
        def _():
            for c in pairs:
                c[1].start()

    def arrive(pairs):
        @pl.when(low_tile)
        def _():
            for c in pairs:
                c[0].wait_recv()

        @pl.when(high_tile)
        def _():
            for c in pairs:
                c[1].wait_recv()

    def left(pairs):
        @pl.when(high_tile)
        def _():
            for c in pairs:
                c[0].wait_send()

        @pl.when(low_tile)
        def _():
            for c in pairs:
                c[1].wait_send()

    start(first)
    nxt = pltpu.make_async_remote_copy(
        src_ref=TT, dst_ref=NT, send_sem=nxt_s, recv_sem=nxt_r,
        device_id={"win": w - 1, "tile": t}, device_id_type=MESH)

    @pl.when(w > 0)
    def _():
        nxt.start()

    def state(k, r, f):
        return get(B0, PAD + r, f, BW) if k == 0 else get(X.at[k - 1], PAD + r, f)

    def side_ok(r):
        return low_ok if r < 0 else high_ok if r >= OWN else None

    def forward(k, blocks):
        outs = []
        for block in blocks:
            near = range(block[0] - 1, block[-1] + 2)
            s = {r: [state(k, r, f) for f in range(NF)] for r in near}
            p = {r: (s[r][4], s[r][4] + s[r][5]) for r in near}
            mass = {r: [get(B0, PAD + r, 6 + l, BW) + s[r][4 + l] for l in range(2)] for r in near}
            q = {r: [mass[r][l] * s[r][2 + l] for l in range(2)] for r in near}
            for r in block:
                cor = COR[pl.ds(PAD + r, 1), :]
                new, dx = [None] * NF, [None] * 4
                lo, hi = r - 1, r + 1
                for l in range(2):
                    u, v, h = s[r][l], s[r][2 + l], s[r][4 + l]
                    dx[l], dx[2 + l] = along_x(u), along_x(v)
                    new[l] = u - HALF_C * (u * dx[l] + v * (s[hi][l] - s[lo][l]) + along_x(p[r][l])) + cor * v
                    new[2 + l] = v - HALF_C * (
                        u * dx[2 + l] + v * (s[hi][2 + l] - s[lo][2 + l]) + (p[hi][l] - p[lo][l])) - cor * u
                    new[4 + l] = h - HALF_C * (along_x(mass[r][l] * u) + (q[hi][l] - q[lo][l]))
                ok = side_ok(r)
                for f in range(NF):
                    new[f] = new[f] + get(B0, PAD + r, 8 + f, BW)
                    if ok is not None:
                        new[f] = new[f] * ok
                outs.append((r, new, dx))
        for r, new, dx in outs:
            for f in range(NF):
                put(X.at[k], PAD + r, f, new[f])
            for f in range(4):
                put(DX.at[k], PAD + r, f, dx[f], 4)

    for k in range(3):
        forward(k, [range(1 + k, OWN - 1 - k)])
    for n, near in enumerate((1, 3, 5)):
        arrive([first[n]] if n < 2 else first[2:])
        if n == 0:
            for c in ins[3:]:
                c.wait()
            spread(OS, 0, 1, 0, lambda cols: TS[:, cols])
            spread(OW, 0, 1, 0, lambda cols: TW[:, cols])
            for l in range(2):
                spread(OV, 0, 2, l, lambda cols: TV[l, :, cols])
        for k in range(STEPS):
            low = [r for r in (k - near, k - near + 1) if r < OWN // 2]
            high = [OWN - 1 - r for r in reversed(low)]
            if low:
                forward(k, [low, high])

    not_last = jnp.where(w < win_n - 1, 1.0, 0.0)

    @pl.when(w < win_n - 1)
    def _():
        nxt.wait_recv()

    @pl.when(w == win_n - 1)
    def _():
        NT[...] = jnp.zeros_like(NT)

    for f in range(NF):
        spread(NXT, 0, NF, f, lambda cols: NT[f // 2, f % 2, :, cols])

    def pull(k, r, l):
        ow = jnp.where(get(OS, r, 0, 1) == k, get(OW, r, 0, 1), 0.0)
        return ow * (state(k, r, 4 + l) - get(OV, r, l, 2))

    for r in range(OWN):
        for f in range(NF):
            mis = (ew[f % 2, f // 2] * not_last) * (get(NXT, r, f) - state(STEPS, r, f))
            put(MU, r, f, mis)
            lam = -mis
            if f >= 4:
                lam = lam + pull(STEPS, r, f - 4)
            put(LAM.at[0], PAD + r, f, lam)
            put(G, GP + r, f, lam)
    mu = pltpu.make_async_remote_copy(
        src_ref=MU, dst_ref=EARL, send_sem=mu_s, recv_sem=mu_r,
        device_id={"win": w + 1, "tile": t}, device_id_type=MESH)

    @pl.when(w < win_n - 1)
    def _():
        mu.start()

    def backward(k, rows):
        src, dst = LAM.at[STEPS - k], LAM.at[STEPS - k + 1]
        reach = STEPS - k
        none = [None] * NF
        near = range(rows[0] - 1, rows[-1] + 2)
        lam = {r: [get(src, PAD + r, f) for f in range(NF)] if -reach <= r < OWN + reach else none for r in near}
        s = {r: [state(k - 1, r, f) for f in range(NF)] for r in near if -reach - 1 <= r < OWN + reach + 1}

        def times(r, l, c):
            return None if lam[r][c] is None else s[r][2 + l] * lam[r][c]

        va = {r: [times(r, l, l) for l in range(2)] for r in near}
        vb = {r: [times(r, l, 2 + l) for l in range(2)] for r in near}
        outs = []
        for r in rows:
            lo, hi = r - 1, r + 1
            new, grads = [None] * NF, [None] * 2
            cor = COR[pl.ds(PAD + r, 1), :]
            for l in range(2):
                u, v, h = s[r][l], s[r][2 + l], s[r][4 + l]
                a, b, c = lam[r][l], lam[r][2 + l], lam[r][4 + l]
                mass = get(B0, PAD + r, 6 + l, BW) + h
                cy = less(lam[hi][4 + l], lam[lo][4 + l])
                ya, yb = less(va[hi][l], va[lo][l]), less(vb[hi][l], vb[lo][l])
                by = less(lam[hi][2 + l], lam[lo][2 + l])
                if a is None:
                    new[l] = HALF_C * ya
                    new[2 + l] = HALF_C * (yb + mass * cy)
                    new[4 + l] = HALF_C * (v * cy)
                    grads[l] = by
                    continue
                cx = along_x(c)
                dxu, dxv = get(DX.at[k - 1], PAD + r, l, 4), get(DX.at[k - 1], PAD + r, 2 + l, 4)
                new[l] = a - cor * b - HALF_C * (a * dxu + b * dxv - along_x(u * a) - ya - mass * cx)
                new[2 + l] = b + cor * a - HALF_C * (
                    a * (s[hi][l] - s[lo][l]) + b * (s[hi][2 + l] - s[lo][2 + l]) - along_x(u * b) - yb - mass * cy)
                new[4 + l] = c + HALF_C * (u * cx + v * cy)
                grads[l] = along_x(a) + by
            new[4] = new[4] + HALF_C * (grads[0] + grads[1])
            new[5] = new[5] + HALF_C * grads[1]
            ok = side_ok(r)
            if k > 1 and ok is None:
                for l in range(2):
                    new[4 + l] = new[4 + l] + pull(k - 1, r, l)
            if ok is not None:
                new = [value * ok for value in new]
            outs.append((r, new))
        for r, new in outs:
            fresh = r == -reach - 1 or r == OWN + reach
            for f in range(NF):
                put(dst, PAD + r, f, new[f])
                if k > 1:
                    put(G, GP + r, f, new[f] if fresh else get(G, GP + r, f) + new[f])

    backward(STEPS, range(-1, OWN + 1))
    for k in range(STEPS - 1, 1, -1):
        reach = STEPS - k + 1
        backward(k, range(-reach, k - 2))
        backward(k, range(OWN + 2 - k, OWN + reach))
    CH = OWN * RW // win_n
    HALO = 2 * (STEPS - 1)
    mine = pl.ds(pl.multiple_of(w * CH, SUB), CH)

    SIZE = OWN * RW

    def add_up(at, p, tile, group, n):
        pltpu.make_async_remote_copy(
            src_ref=G.at[pl.ds(pl.multiple_of(GP * RW + at, SUB), CH), :],
            dst_ref=RS.at[pl.ds(group * SIZE + n * CH, CH), :],
            send_sem=rs_s[group], recv_sem=rs_r[group],
            device_id={"win": p, "tile": tile}, device_id_type=MESH).start()

    every = peers + [(0, 0)]

    def up_to(n, p):
        @pl.when(p < HALO)
        def _():
            add_up(SIZE + p * CH, p, t + 1, 1, n)

    def down_to(n, p):
        @pl.when(p >= win_n - HALO)
        def _():
            add_up(p * CH - SIZE, p, t - 1, 2, n)

    @pl.when(high_tile)
    def _():
        for n, (a, b) in enumerate(every):
            up_to(n, peer(a, b))

    @pl.when(low_tile)
    def _():
        for n, (a, b) in enumerate(every):
            down_to(n, peer(a, b))

    for k in range(STEPS - 1, 1, -1):
        backward(k, range(k - 2, OWN + 2 - k))

    for n, (a, b) in enumerate(peers):
        p = peer(a, b)
        add_up(p * CH, p, t, 0, n)
    backward(1, range(-STEPS, OWN // 2))
    backward(1, range(OWN // 2, OWN + STEPS))
    last = LAM.at[STEPS]
    lam_halo = [
        to_tile(last, (PAD + OWN) * RW, LH.at[0], 0, PAD * RW, (h_s, h_r), 0, 0),
        to_tile(last, 0, LH.at[1], 0, PAD * RW, (h_s, h_r), 0, 1)]
    start([lam_halo])

    def all_of(ref, count, sem):
        part = ref.at[pl.ds(0, count * CH), :]
        pltpu.make_async_copy(part, part, sem).wait()

    def take(group, count):
        all_of(RS, count, rs_r[group])
        total = RED[...]
        for n in range(count):
            total = total + RS[pl.ds(group * SIZE + n * CH, CH), :]
        RED[...] = total

    RED[...] = G[pl.ds(pl.multiple_of(GP * RW + w * CH, SUB), CH), :]
    take(0, win_n - 1)

    @pl.when(low_tile)
    def _():
        @pl.when(w < HALO)
        def _():
            take(1, win_n)

    @pl.when(high_tile)
    def _():
        @pl.when(w >= win_n - HALO)
        def _():
            take(2, win_n)

    for a, b in peers:
        pltpu.make_async_remote_copy(
            src_ref=RED, dst_ref=AG.at[mine, :], send_sem=ag_s, recv_sem=ag_r,
            device_id={"win": peer(a, b), "tile": t}, device_id_type=MESH).start()
    AG[mine, :] = RED[...]

    arrive([lam_halo])

    def add_rows(at, src):
        span = pl.ds(at * RW, PAD * RW)
        last[span, :] = last[span, :] + src[...]

    @pl.when(low_tile)
    def _():
        add_rows(PAD, LH.at[0])

    @pl.when(high_tile)
    def _():
        add_rows(PAD + OWN - PAD, LH.at[1])

    @pl.when(w > 0)
    def _():
        mu.wait_recv()

    @pl.when(w == 0)
    def _():
        EARL[...] = jnp.zeros_like(EARL)

    def gather(src, first, f, s):
        return src[pl.ds((first * NF + f) * SUB + s, OWN, stride=RW), :]

    for f in range(NF):
        for s in range(SUB):
            gs_out[0, f // 2, f % 2, :, pl.ds(128 * s, 128)] = (
                gather(last, PAD, f, s) + gather(EARL, 0, f, s))

    all_of(AG, win_n - 1, ag_r)
    for f in range(NF):
        for s in range(SUB):
            gf_out[f // 2, f % 2, :, pl.ds(128 * s, 128)] = gather(AG, 0, f, s)

    left(first + [lam_halo])

    @pl.when(w > 0)
    def _():
        nxt.wait_send()

    @pl.when(w < win_n - 1)
    def _():
        mu.wait_send()

    all_of(RS, win_n - 1, rs_s[0])

    @pl.when(high_tile)
    def _():
        all_of(RS, HALO, rs_s[1])

    @pl.when(low_tile)
    def _():
        all_of(RS, HALO, rs_s[2])

    all_of(RS, win_n - 1, ag_s)


def hand_over(a, b, a_out, b_out, sems):
    copies = [pltpu.make_async_copy(src, dst, sems.at[n]) for n, (src, dst) in enumerate([(a, a_out), (b, b_out)])]
    for c in copies:
        c.start()
    for c in copies:
        c.wait()


def solution(mesh):
    win_n, tile_n = mesh.shape["win"], mesh.shape["tile"]

    def local(traj, forc, dep, ostep, oval, owt, ew):
        f32 = jnp.float32

        def flat(rows, width, dtype=f32, lead=()):
            return pltpu.VMEM(lead + (rows * width * SUB, 128), dtype)

        vm = pl.BlockSpec(memory_space=pltpu.VMEM)
        hbm = pl.BlockSpec(memory_space=pltpu.HBM)
        sem = pltpu.SemaphoreType.DMA
        results = pl.pallas_call(
            functools.partial(kernel, win_n, tile_n),
            out_shape=(jax.ShapeDtypeStruct(traj.shape, f32), jax.ShapeDtypeStruct(forc.shape, f32)),
            in_specs=[hbm] * 7,
            out_specs=(vm, vm),
            scratch_shapes=[
                pltpu.VMEM(traj.shape[1:], f32), pltpu.VMEM(forc.shape, f32), pltpu.VMEM(dep.shape, f32),
                pltpu.VMEM(ostep.shape[1:], jnp.int32), pltpu.VMEM(oval.shape[1:], f32),
                pltpu.VMEM(owt.shape, f32), pltpu.SMEM((2, 3), f32),
                flat(ROWS, BW),
                flat(ROWS, NF, lead=(STEPS,)),
                flat(ROWS, 4, lead=(STEPS,)),
                flat(OWN + 1, 1, jnp.int32),
                flat(OWN + 1, 2),
                flat(OWN + 1, 1),
                pltpu.VMEM((24, 128), f32),
                pltpu.VMEM(traj.shape[1:], f32),
                flat(OWN + 1, NF),
                flat(OWN, NF),
                flat(OWN, NF),
                flat(ROWS, NF, lead=(STEPS + 1,)),
                flat(OWN + 2 * GP, NF),
                flat(PAD, NF, lead=(2,)),
                flat(3 * OWN, NF),
                pltpu.VMEM((OWN * RW // win_n, 128), f32),
                flat(OWN, NF),
                sem((7,)), sem((4, 2)), sem((4, 2)), sem, sem, sem, sem, sem((1, 2)), sem((1, 2)),
                sem, sem, sem, sem, sem, sem, sem, sem,
            ],
            compiler_params=pltpu.CompilerParams(
                collective_id=0, has_side_effects=True, vmem_limit_bytes=16 * 2**20),
        )(*[pltpu.with_memory_space_constraint(z, pltpu.HBM) for z in (traj, forc, dep, ostep, oval, owt, ew.T)])
        return pl.pallas_call(
            hand_over,
            out_shape=[jax.ShapeDtypeStruct(r.shape, f32) for r in results],
            in_specs=[vm] * 2,
            out_specs=[hbm] * 2,
            scratch_shapes=[sem((2,))],
        )(*results)

    return jax.shard_map(
        local,
        mesh=mesh,
        in_specs=(
            P("win", None, None, "tile", None),
            P(None, None, "tile", None),
            P(None, "tile", None),
            P("win", "tile", None),
            P("win", None, "tile", None),
            P("tile", None),
            P(),
        ),
        out_specs=(P("win", None, None, "tile", None), P(None, None, "tile", None)),
        check_vma=False,
    )
```

```python
import functools

import jax
import jax.numpy as jnp
from jax import lax
from jax.experimental import pallas as pl
from jax.experimental.pallas import tpu as pltpu
from jax.sharding import PartitionSpec as P

MESH = pl.DeviceIdType.MESH
STEPS = 6
LAT_ROWS = 2048
C_STEP = 0.2
HALF_C = 0.1
OWN = 8
PAD = STEPS
ROWS = OWN + 2 * PAD
NF = 6
SUB = 8
RW = NF * SUB
BW = 14
BR = BW * SUB


def along_x(a):
    lane = lax.broadcasted_iota(jnp.int32, a.shape, 1)
    up = pltpu.roll(a, 127, 1)
    up = jnp.where(lane == 127, pltpu.roll(up, SUB - 1, 0), up)
    down = pltpu.roll(a, 1, 1)
    down = jnp.where(lane == 0, pltpu.roll(down, 1, 0), down)
    return up - down


def get(ref, row, f, width=NF):
    return ref[pl.ds((row * width + f) * SUB, SUB), :]


def put(ref, row, f, value, width=NF):
    ref[pl.ds((row * width + f) * SUB, SUB), :] = value


def less(a, b):
    if a is None:
        return None if b is None else -b
    return a if b is None else a - b


def kernel(
    win_n, tile_n, traj, forc, dep, ostep, oval, owt, ew_in,
    gs_out, gf_out,
    TT, TF, TD, TS, TV, TW, ew,
    B0, X, DX, OS, OV, OW, COR, NT, NXT, MU, EARL, LAM, G, GH, LH, RS, RED, AG,
    in_s, init_s, init_r, nxt_s, nxt_r, mu_s, mu_r, h_s, h_r, rs_s, rs_r, ag_s, ag_r,
):
    w = lax.axis_index("win")
    t = lax.axis_index("tile")
    y, x = w // 4, lax.rem(w, 4)
    low_tile, high_tile = t > 0, t < tile_n - 1

    def peer(a, b):
        return lax.rem(y + a, 4) * 4 + lax.rem(x + b, 4)

    peers = [(a, b) for a in range(4) for b in range(4) if a or b]
    peers.sort(key=lambda p: -(min(p[0], 4 - p[0]) + min(p[1], 4 - p[1])))

    barrier = pltpu.get_barrier_semaphore()

    def greet(win, tile):
        pl.semaphore_signal(barrier, inc=1, device_id={"win": win, "tile": tile}, device_id_type=MESH)

    @pl.when(low_tile)
    def _():
        greet(w, t - 1)

    @pl.when(high_tile)
    def _():
        greet(w, t + 1)

    ins = [pltpu.make_async_copy(src, dst, in_s.at[n]) for n, (src, dst) in enumerate(
        [(traj.at[0], TT), (dep, TD), (forc, TF), (ostep.at[0], TS), (oval.at[0], TV), (owt, TW), (ew_in, ew)])]
    for c in ins:
        c.start()

    for a, b in peers:
        greet(peer(a, b), t)

    band_row = lax.broadcasted_iota(jnp.int32, (24, 128), 0) + (t * OWN - PAD)
    lat = ((LAT_ROWS - tile_n * OWN) // 2 + band_row).astype(jnp.float32)
    COR[...] = (2.0 * C_STEP) * jnp.sin(jnp.pi * ((lat + 0.5) / LAT_ROWS - 0.5))
    low_ok = jnp.where(low_tile, 1.0, 0.0)
    high_ok = jnp.where(high_tile, 1.0, 0.0)

    @pl.when(t == 0)
    def _():
        B0[pl.ds(0, PAD * BR), :] = jnp.zeros((PAD * BR, 128), jnp.float32)

    @pl.when(t == tile_n - 1)
    def _():
        B0[pl.ds((PAD + OWN) * BR, PAD * BR), :] = jnp.zeros((PAD * BR, 128), jnp.float32)

    def spread(dst, first, width, f, tile):
        for s in range(SUB):
            dst[pl.ds((first * width + f) * SUB + s, OWN, stride=width * SUB), :] = tile(pl.ds(128 * s, 128))

    ins[0].wait()
    for f in range(NF):
        spread(B0, PAD, BW, f, lambda cols: TT[f // 2, f % 2, :, cols])
    ins[1].wait()
    for l in range(2):
        spread(B0, PAD, BW, 6 + l, lambda cols: TD[l, :, cols])
    ins[2].wait()
    for f in range(NF):
        spread(B0, PAD, BW, 8 + f, lambda cols: TF[f // 2, f % 2, :, cols])

    pl.semaphore_wait(barrier, win_n - 1 + jnp.where(low_tile, 1, 0) + jnp.where(high_tile, 1, 0))

    def to_tile(src, src_at, dst, dst_at, size, sems, n, side):
        return pltpu.make_async_remote_copy(
            src_ref=src.at[pl.ds(src_at, size), :], dst_ref=dst.at[pl.ds(dst_at, size), :],
            send_sem=sems[0].at[n, side], recv_sem=sems[1].at[n, side],
            device_id={"win": w, "tile": t + 1 if side == 0 else t - 1}, device_id_type=MESH)

    def init(n, near, count, size):
        up = (PAD + OWN - near - count + 1) * BR, (PAD - near - count + 1) * BR
        down = (PAD + near - 1) * BR, (PAD + OWN + near - 1) * BR
        return [to_tile(B0, a, B0, b, size, (init_s, init_r), n, side) for side, (a, b) in enumerate((up, down))]

    first = [init(0, 1, 2, 2 * BR), init(1, 3, 2, 2 * BR), init(2, 5, 1, BR), init(3, 6, 1, SUB * SUB)]

    def start(pairs):
        @pl.when(high_tile)
        def _():
            for c in pairs:
                c[0].start()

        @pl.when(low_tile)
        def _():
            for c in pairs:
                c[1].start()

    def arrive(pairs):
        @pl.when(low_tile)
        def _():
            for c in pairs:
                c[0].wait_recv()

        @pl.when(high_tile)
        def _():
            for c in pairs:
                c[1].wait_recv()

    def left(pairs):
        @pl.when(high_tile)
        def _():
            for c in pairs:
                c[0].wait_send()

        @pl.when(low_tile)
        def _():
            for c in pairs:
                c[1].wait_send()

    start(first)
    nxt = pltpu.make_async_remote_copy(
        src_ref=TT, dst_ref=NT, send_sem=nxt_s, recv_sem=nxt_r,
        device_id={"win": w - 1, "tile": t}, device_id_type=MESH)

    @pl.when(w > 0)
    def _():
        nxt.start()

    def state(k, r, f):
        return get(B0, PAD + r, f, BW) if k == 0 else get(X.at[k - 1], PAD + r, f)

    def side_ok(r):
        return low_ok if r < 0 else high_ok if r >= OWN else None

    def forward(k, blocks):
        outs = []
        for block in blocks:
            near = range(block[0] - 1, block[-1] + 2)
            s = {r: [state(k, r, f) for f in range(NF)] for r in near}
            p = {r: (s[r][4], s[r][4] + s[r][5]) for r in near}
            mass = {r: [get(B0, PAD + r, 6 + l, BW) + s[r][4 + l] for l in range(2)] for r in near}
            q = {r: [mass[r][l] * s[r][2 + l] for l in range(2)] for r in near}
            for r in block:
                cor = COR[pl.ds(PAD + r, 1), :]
                new, dx = [None] * NF, [None] * 4
                lo, hi = r - 1, r + 1
                for l in range(2):
                    u, v, h = s[r][l], s[r][2 + l], s[r][4 + l]
                    dx[l], dx[2 + l] = along_x(u), along_x(v)
                    new[l] = u - HALF_C * (u * dx[l] + v * (s[hi][l] - s[lo][l]) + along_x(p[r][l])) + cor * v
                    new[2 + l] = v - HALF_C * (
                        u * dx[2 + l] + v * (s[hi][2 + l] - s[lo][2 + l]) + (p[hi][l] - p[lo][l])) - cor * u
                    new[4 + l] = h - HALF_C * (along_x(mass[r][l] * u) + (q[hi][l] - q[lo][l]))
                ok = side_ok(r)
                for f in range(NF):
                    new[f] = new[f] + get(B0, PAD + r, 8 + f, BW)
                    if ok is not None:
                        new[f] = new[f] * ok
                outs.append((r, new, dx))
        for r, new, dx in outs:
            for f in range(NF):
                put(X.at[k], PAD + r, f, new[f])
            for f in range(4):
                put(DX.at[k], PAD + r, f, dx[f], 4)

    for k in range(3):
        forward(k, [range(1 + k, OWN - 1 - k)])
    for n, near in enumerate((1, 3, 5)):
        arrive([first[n]] if n < 2 else first[2:])
        if n == 0:
            for c in ins[3:]:
                c.wait()
            spread(OS, 0, 1, 0, lambda cols: TS[:, cols])
            spread(OW, 0, 1, 0, lambda cols: TW[:, cols])
            for l in range(2):
                spread(OV, 0, 2, l, lambda cols: TV[l, :, cols])
        for k in range(STEPS):
            low = [r for r in (k - near, k - near + 1) if r < OWN // 2]
            high = [OWN - 1 - r for r in reversed(low)]
            if low:
                forward(k, [low, high])

    not_last = jnp.where(w < win_n - 1, 1.0, 0.0)

    @pl.when(w < win_n - 1)
    def _():
        nxt.wait_recv()

    @pl.when(w == win_n - 1)
    def _():
        NT[...] = jnp.zeros_like(NT)

    for f in range(NF):
        spread(NXT, 0, NF, f, lambda cols: NT[f // 2, f % 2, :, cols])

    def pull(k, r, l):
        ow = jnp.where(get(OS, r, 0, 1) == k, get(OW, r, 0, 1), 0.0)
        return ow * (state(k, r, 4 + l) - get(OV, r, l, 2))

    for r in range(OWN):
        for f in range(NF):
            mis = (ew[f % 2, f // 2] * not_last) * (get(NXT, r, f) - state(STEPS, r, f))
            put(MU, r, f, mis)
            lam = -mis
            if f >= 4:
                lam = lam + pull(STEPS, r, f - 4)
            put(LAM.at[0], PAD + r, f, lam)
            put(G, PAD + r, f, lam)
    mu = pltpu.make_async_remote_copy(
        src_ref=MU, dst_ref=EARL, send_sem=mu_s, recv_sem=mu_r,
        device_id={"win": w + 1, "tile": t}, device_id_type=MESH)

    @pl.when(w < win_n - 1)
    def _():
        mu.start()

    def backward(k, rows):
        src, dst = LAM.at[STEPS - k], LAM.at[STEPS - k + 1]
        reach = STEPS - k
        none = [None] * NF
        near = range(rows[0] - 1, rows[-1] + 2)
        lam = {r: [get(src, PAD + r, f) for f in range(NF)] if -reach <= r < OWN + reach else none for r in near}
        s = {r: [state(k - 1, r, f) for f in range(NF)] for r in near if -reach - 1 <= r < OWN + reach + 1}

        def times(r, l, c):
            return None if lam[r][c] is None else s[r][2 + l] * lam[r][c]

        va = {r: [times(r, l, l) for l in range(2)] for r in near}
        vb = {r: [times(r, l, 2 + l) for l in range(2)] for r in near}
        outs = []
        for r in rows:
            lo, hi = r - 1, r + 1
            new, grads = [None] * NF, [None] * 2
            cor = COR[pl.ds(PAD + r, 1), :]
            for l in range(2):
                u, v, h = s[r][l], s[r][2 + l], s[r][4 + l]
                a, b, c = lam[r][l], lam[r][2 + l], lam[r][4 + l]
                mass = get(B0, PAD + r, 6 + l, BW) + h
                cy = less(lam[hi][4 + l], lam[lo][4 + l])
                ya, yb = less(va[hi][l], va[lo][l]), less(vb[hi][l], vb[lo][l])
                by = less(lam[hi][2 + l], lam[lo][2 + l])
                if a is None:
                    new[l] = HALF_C * ya
                    new[2 + l] = HALF_C * (yb + mass * cy)
                    new[4 + l] = HALF_C * (v * cy)
                    grads[l] = by
                    continue
                cx = along_x(c)
                dxu, dxv = get(DX.at[k - 1], PAD + r, l, 4), get(DX.at[k - 1], PAD + r, 2 + l, 4)
                new[l] = a - cor * b - HALF_C * (a * dxu + b * dxv - along_x(u * a) - ya - mass * cx)
                new[2 + l] = b + cor * a - HALF_C * (
                    a * (s[hi][l] - s[lo][l]) + b * (s[hi][2 + l] - s[lo][2 + l]) - along_x(u * b) - yb - mass * cy)
                new[4 + l] = c + HALF_C * (u * cx + v * cy)
                grads[l] = along_x(a) + by
            new[4] = new[4] + HALF_C * (grads[0] + grads[1])
            new[5] = new[5] + HALF_C * grads[1]
            ok = side_ok(r)
            if k > 1 and ok is None:
                for l in range(2):
                    new[4 + l] = new[4 + l] + pull(k - 1, r, l)
            if ok is not None:
                new = [value * ok for value in new]
            outs.append((r, new))
        for r, new in outs:
            fresh = r == -reach - 1 or r == OWN + reach
            for f in range(NF):
                put(dst, PAD + r, f, new[f])
                if k > 1:
                    put(G, PAD + r, f, new[f] if fresh else get(G, PAD + r, f) + new[f])

    backward(STEPS, range(-1, OWN + 1))
    for k in range(STEPS - 1, 1, -1):
        reach = STEPS - k + 1
        backward(k, range(-reach, k - 2))
        backward(k, range(OWN + 2 - k, OWN + reach))
    g_halo = [
        to_tile(G, (PAD + OWN) * RW, GH.at[0], 0, (PAD - 1) * RW, (h_s, h_r), 1, 0),
        to_tile(G, RW, GH.at[1], 0, (PAD - 1) * RW, (h_s, h_r), 1, 1)]
    start([g_halo])
    for k in range(STEPS - 1, 1, -1):
        backward(k, range(k - 2, OWN + 2 - k))
    backward(1, range(-STEPS, OWN // 2))
    backward(1, range(OWN // 2, OWN + STEPS))
    last = LAM.at[STEPS]
    lam_halo = [
        to_tile(last, (PAD + OWN) * RW, LH.at[0], 0, PAD * RW, (h_s, h_r), 0, 0),
        to_tile(last, 0, LH.at[1], 0, PAD * RW, (h_s, h_r), 0, 1)]
    start([lam_halo])

    CH = OWN * RW // win_n

    def chunk(p):
        return pl.ds(pl.multiple_of(PAD * RW + p * CH, SUB), CH)

    def add_halo(at, src):
        span = pl.ds(at * RW, (PAD - 1) * RW)
        G[span, :] = G[span, :] + src[...]

    def from_low():
        g_halo[0].wait_recv()
        add_halo(PAD, GH.at[0])

    def from_high():
        g_halo[1].wait_recv()
        add_halo(PAD + OWN - PAD + 1, GH.at[1])

    def to_sum(p, n):
        pltpu.make_async_remote_copy(
            src_ref=G.at[chunk(p), :], dst_ref=RS.at[pl.ds(n * CH, CH), :], send_sem=rs_s, recv_sem=rs_r,
            device_id={"win": p, "tile": t}, device_id_type=MESH).start()

    def to_sums(wanted):
        for n, (a, b) in enumerate(peers):
            p = peer(a, b)
            pl.when(wanted(p))(functools.partial(to_sum, p, n))

    alone = 2 * (OWN - (PAD - 1))
    core = lax.rem(t, 2)

    @pl.when(core == 0)
    def _():
        from_high()
        to_sums(lambda p: p >= win_n - alone)
        pl.when(low_tile)(from_low)
        to_sums(lambda p: p < win_n - alone)

    @pl.when(core == 1)
    def _():
        from_low()
        to_sums(lambda p: p < alone)
        pl.when(high_tile)(from_high)
        to_sums(lambda p: p >= alone)

    def all_of(ref, count, sem):
        part = ref.at[pl.ds(0, count * CH), :]
        pltpu.make_async_copy(part, part, sem).wait()

    all_of(RS, win_n - 1, rs_r)
    total = G[chunk(w), :]
    for n in range(win_n - 1):
        total = total + RS[pl.ds(n * CH, CH), :]
    RED[...] = total

    mine = pl.ds(pl.multiple_of(w * CH, SUB), CH)
    for a, b in peers:
        pltpu.make_async_remote_copy(
            src_ref=RED, dst_ref=AG.at[mine, :], send_sem=ag_s, recv_sem=ag_r,
            device_id={"win": peer(a, b), "tile": t}, device_id_type=MESH).start()
    AG[mine, :] = RED[...]

    arrive([lam_halo])

    def add_rows(at, src):
        span = pl.ds(at * RW, PAD * RW)
        last[span, :] = last[span, :] + src[...]

    @pl.when(low_tile)
    def _():
        add_rows(PAD, LH.at[0])

    @pl.when(high_tile)
    def _():
        add_rows(PAD + OWN - PAD, LH.at[1])

    @pl.when(w > 0)
    def _():
        mu.wait_recv()

    @pl.when(w == 0)
    def _():
        EARL[...] = jnp.zeros_like(EARL)

    def gather(src, first, f, s):
        return src[pl.ds((first * NF + f) * SUB + s, OWN, stride=RW), :]

    for f in range(NF):
        for s in range(SUB):
            gs_out[0, f // 2, f % 2, :, pl.ds(128 * s, 128)] = (
                gather(last, PAD, f, s) + gather(EARL, 0, f, s))

    all_of(AG, win_n - 1, ag_r)
    for f in range(NF):
        for s in range(SUB):
            gf_out[f // 2, f % 2, :, pl.ds(128 * s, 128)] = gather(AG, 0, f, s)

    left(first + [lam_halo, g_halo])

    @pl.when(w > 0)
    def _():
        nxt.wait_send()

    @pl.when(w < win_n - 1)
    def _():
        mu.wait_send()

    all_of(RS, win_n - 1, rs_s)
    all_of(RS, win_n - 1, ag_s)


def solution(mesh):
    win_n, tile_n = mesh.shape["win"], mesh.shape["tile"]

    def local(traj, forc, dep, ostep, oval, owt, ew):
        f32 = jnp.float32

        def flat(rows, width, dtype=f32, lead=()):
            return pltpu.VMEM(lead + (rows * width * SUB, 128), dtype)

        vm = pl.BlockSpec(memory_space=pltpu.VMEM)
        hbm = pl.BlockSpec(memory_space=pltpu.HBM)
        sem = pltpu.SemaphoreType.DMA
        return pl.pallas_call(
            functools.partial(kernel, win_n, tile_n),
            out_shape=(jax.ShapeDtypeStruct(traj.shape, f32), jax.ShapeDtypeStruct(forc.shape, f32)),
            in_specs=[hbm] * 7,
            out_specs=(vm, vm),
            scratch_shapes=[
                pltpu.VMEM(traj.shape[1:], f32), pltpu.VMEM(forc.shape, f32), pltpu.VMEM(dep.shape, f32),
                pltpu.VMEM(ostep.shape[1:], jnp.int32), pltpu.VMEM(oval.shape[1:], f32),
                pltpu.VMEM(owt.shape, f32), pltpu.SMEM((2, 3), f32),
                flat(ROWS, BW),
                flat(ROWS, NF, lead=(STEPS,)),
                flat(ROWS, 4, lead=(STEPS,)),
                flat(OWN + 1, 1, jnp.int32),
                flat(OWN + 1, 2),
                flat(OWN + 1, 1),
                pltpu.VMEM((24, 128), f32),
                pltpu.VMEM(traj.shape[1:], f32),
                flat(OWN + 1, NF),
                flat(OWN, NF),
                flat(OWN, NF),
                flat(ROWS, NF, lead=(STEPS + 1,)),
                flat(ROWS, NF),
                flat(PAD - 1, NF, lead=(2,)),
                flat(PAD, NF, lead=(2,)),
                flat(OWN, NF),
                pltpu.VMEM((OWN * RW // win_n, 128), f32),
                flat(OWN, NF),
                sem((7,)), sem((4, 2)), sem((4, 2)), sem, sem, sem, sem, sem((2, 2)), sem((2, 2)),
                sem, sem, sem, sem,
            ],
            compiler_params=pltpu.CompilerParams(
                collective_id=0, has_side_effects=True, vmem_limit_bytes=16 * 2**20),
        )(*[pltpu.with_memory_space_constraint(z, pltpu.HBM) for z in (traj, forc, dep, ostep, oval, owt, ew.T)])

    return jax.shard_map(
        local,
        mesh=mesh,
        in_specs=(
            P("win", None, None, "tile", None),
            P(None, None, "tile", None),
            P(None, "tile", None),
            P("win", "tile", None),
            P("win", None, "tile", None),
            P("tile", None),
            P(),
        ),
        out_specs=(P("win", None, None, "tile", None), P(None, None, "tile", None)),
        check_vma=False,
    )
```
